512 devices in a mesh: leaf: 128 (over z, y, core), vec: 4 (over x).
Axes of the slice: x: 4, y: 8, z: 8, core: 2. Of those that a mesh axis runs over, the one named last changes fastest.
Arguments:
- vectors: float32 [64, 524288], P('vec', 'leaf'), may hold values from -6 to 6
- points: float32 [2, 524288], P(None, 'leaf'), may hold values from 0 to 1
- bases: float32 [2048, 256, 64], P('leaf'), may hold values from -0.375 to 0.375
- transfer: float32 [6, 2, 64, 64], replicated, may hold values from -0.5 to 0.5
- coupling: float32 [7, 4, 64, 64], replicated, may hold values from -0.375 to 0.375
- near_lists: int32 [2048, 8], P('leaf'), may hold values from 0 to 2047, as said below
- far_lists: int32 [4, 2048, 4], P(None, 'leaf'), may hold values from 0 to 2047, as said below
- coarse_lists: int32 [3, 128, 4], replicated, may hold values from 0 to 127, as said below
Outputs:
- product: float32 [64, 524288], P('vec', 'leaf')
The draws below stay inside these ranges and needn't reach their ends.
Inputs may be any that keep to these rules, and one draw needn't show every extreme that they name: `near_lists`: row l lists 8 leaves other than l, each within 16 leaves of l. Row d * 16 + j with j below 16 / 2**k of far_lists[k] belongs to node d * (16 / 2**k) + j of level k and lists other nodes of that level within 16 / 2**k of it; all other rows are 0. Row n of coarse_lists[i] for n below 128 / 2**i lists nodes of level 4 + i, any of them; all other rows are 0.
All inputs are finite; a program needn't handle non-finite values.
Results may differ from the reference program's by a relative error of at most 0.0003.
Values sent between devices are 32-bit elements; how exact they have to be, the bound alone decides.
A program may use at most 64 MiB of HBM per device.

```python
import jax
import jax.numpy as jnp
from jax import lax

LEAF = 256
RANK = 64
NVEC = 64
CUT = 4
COARSE = 2
NEAR = 8
FAR = 4
LEAF_DEV = 16
NLEAVES = 2048
POINTS = 524288
LEVELS = 7
N_LEAF = 128


def draw_near_lists(key, part):
    key = jax.random.fold_in(key, 11)
    first, second = jax.random.split(key)
    count = LEAF_DEV * N_LEAF
    dist = jax.random.randint(first, (count, NEAR), 1, LEAF_DEV + 1)
    sign = jax.random.randint(second, (count, NEAR), 0, 2) * 2 - 1
    base = jnp.arange(count, dtype=jnp.int32)[:, None]
    cand = base + sign * dist
    outside = (cand < 0) | (cand >= count)
    return jnp.where(outside, base - sign * dist, cand).astype(jnp.int32)


def draw_far_lists(key, part):
    key = jax.random.fold_in(key, 23)
    first, second = jax.random.split(key)
    level = jnp.arange(CUT, dtype=jnp.int32)[:, None, None]
    row = jnp.arange(LEAF_DEV * N_LEAF, dtype=jnp.int32)[None, :, None]
    span = LEAF_DEV // 2 ** level
    local = row % LEAF_DEV
    node = row // LEAF_DEV * span + local
    total = N_LEAF * span
    shape = (CUT, LEAF_DEV * N_LEAF, FAR)
    dist = jax.random.randint(first, shape, 1, jnp.broadcast_to(span + 1, shape))
    sign = jax.random.randint(second, shape, 0, 2) * 2 - 1
    cand = node + sign * dist
    outside = (cand < 0) | (cand >= total)
    entry = jnp.where(outside, node - sign * dist, cand)
    return jnp.where(local < span, entry, 0).astype(jnp.int32)


def draw_coarse_lists(key, part):
    key = jax.random.fold_in(key, 37)
    level = jnp.arange(COARSE + 1, dtype=jnp.int32)[:, None, None]
    row = jnp.arange(N_LEAF, dtype=jnp.int32)[None, :, None]
    count = N_LEAF // 2 ** level
    shape = (COARSE + 1, N_LEAF, FAR)
    entry = jax.random.randint(key, shape, 0, jnp.broadcast_to(count, shape))
    return jnp.where(row < count, entry, 0).astype(jnp.int32)


def block_scale(rng, dims, cuts, low, largest):
    factor_of = 1.0
    for position, blocks in cuts:
        steps = jax.random.uniform(jax.random.fold_in(jax.random.fold_in(rng, 6), position), (blocks,), jnp.float32, low / len(cuts), largest / len(cuts))
        factor_of = factor_of * jnp.repeat(jnp.exp(steps), dims[position] // blocks).reshape((-1,) + (1,) * (len(dims) - 1 - position))
    return factor_of


def gaussian(stream_key, extent, scale, most, cuts=(), kind=jnp.bfloat16):
    values = scale * jax.random.normal(stream_key, extent, jnp.float32)
    if cuts:
        values = values * block_scale(stream_key, extent, cuts, -0.22, 0.18)
    return jnp.clip(values, -most, most).astype(kind)


def setup_inputs(seed: int = 0) -> dict:
    key_list = jax.random.split(jax.random.key(seed), 9)
    vectors = gaussian(key_list[0], (NVEC, POINTS), 1.0, 6.0, ((0, 4), (1, 128)), jnp.float32)
    points = jnp.clip(1.0 * jax.random.uniform(key_list[1], (2, POINTS), jnp.float32) ** block_scale(key_list[1], (2, POINTS), ((1, 128),), -0.2, 0.2), 0.0, 1.0)
    bases = gaussian(key_list[2], (NLEAVES, LEAF, RANK), LEAF ** -0.5, 0.375, ((0, 128),), jnp.float32)
    transfer = gaussian(key_list[3], (LEVELS - 1, 2, RANK, RANK), (2 * RANK) ** -0.5, 0.5, (), jnp.float32)
    coupling = gaussian(key_list[4], (LEVELS, FAR, RANK, RANK), (FAR * RANK) ** -0.5, 0.375, (), jnp.float32)
    near_lists = draw_near_lists(jax.random.fold_in(key_list[8], 71), 0)
    far_lists = draw_far_lists(jax.random.fold_in(key_list[8], 71), 0)
    coarse_lists = draw_coarse_lists(jax.random.fold_in(key_list[8], 71), 0)
    return dict(vectors=vectors, points=points, bases=bases, transfer=transfer, coupling=coupling, near_lists=near_lists, far_lists=far_lists, coarse_lists=coarse_lists)


highest = lax.Precision.HIGHEST
kernel_width = 0.2
near_weight = 0.0625

def kernel(source, target):
    dx = source[0][:, :, None] - target[0][None, None, :]
    dy = source[1][:, :, None] - target[1][None, None, :]
    return near_weight * jnp.exp(-jnp.sqrt(dx * dx + dy * dy) / kernel_width)

def upward(child, pair):
    grouped = child.reshape(child.shape[0] // 2, 2, child.shape[1], child.shape[2])
    return jnp.einsum('nvr,rs->nvs', grouped[:, 0], pair[0], precision=highest) + jnp.einsum('nvr,rs->nvs', grouped[:, 1], pair[1], precision=highest)

def downward(parent, pair):
    left = jnp.einsum('nvs,rs->nvr', parent, pair[0], precision=highest)
    right = jnp.einsum('nvs,rs->nvr', parent, pair[1], precision=highest)
    return jnp.stack([left, right], 1).reshape(2 * parent.shape[0], parent.shape[1], parent.shape[2])

def far_terms(source, rows, maps):
    total = jnp.einsum('nvr,rs->nvs', source[rows[:, 0]], maps[0], precision=highest)
    for slot in range(1, rows.shape[1]):
        total = total + jnp.einsum('nvr,rs->nvs', source[rows[:, slot]], maps[slot], precision=highest)
    return total

def coarse_pass(cut_up, transfer, coupling, lists, cut):
    ups = [cut_up]
    for level in range(1, lists.shape[0]):
        ups.append(upward(ups[-1], transfer[cut + level - 1]))
    result = None
    for level in range(lists.shape[0] - 1, -1, -1):
        count = ups[level].shape[0]
        here = far_terms(ups[level], lists[level, :count], coupling[cut + level])
        result = here if result is None else here + downward(result, transfer[cut + level])
    return result

def reference(vectors, points, bases, transfer, coupling, near_lists, far_lists, coarse_lists):
    nleaves = bases.shape[0]
    leaf = bases.shape[1]
    cols = vectors.shape[0]
    blocks = vectors.reshape(cols, nleaves, leaf)
    ups = [jnp.einsum('vlp,lpr->lvr', blocks, bases, precision=highest)]
    for level in range(1, CUT + 1):
        ups.append(upward(ups[-1], transfer[level - 1]))
    result = coarse_pass(ups[CUT], transfer, coupling, coarse_lists, CUT)
    for level in range(CUT - 1, -1, -1):
        count = LEAF_DEV >> level
        rows = far_lists[level].reshape(N_LEAF, LEAF_DEV, FAR)[:, :count].reshape(-1, FAR)
        result = far_terms(ups[level], rows, coupling[level]) + downward(result, transfer[level])
    far_part = jnp.einsum('lvr,lpr->vlp', result, bases, precision=highest).reshape(cols, nleaves * leaf)
    wide = jnp.concatenate([vectors, points], 0).reshape(cols + 2, nleaves, leaf)

    def one_leaf(inputs):
        index, row = inputs
        picks = jnp.concatenate([jnp.reshape(index, (1,)).astype(jnp.int32), row.astype(jnp.int32)])
        taken = wide[:, picks, :]
        weights = kernel(taken[cols:], taken[cols:, 0, :])
        return jnp.einsum('vjs,jst->vt', taken[:cols], weights, precision=highest)
    near = lax.map(one_leaf, (jnp.arange(nleaves, dtype=jnp.int32), near_lists))
    return far_part + jnp.transpose(near, (1, 0, 2)).reshape(cols, nleaves * leaf)
```

```python
import jax
import jax.numpy as jnp
from jax import lax
from jax.experimental import pallas as pl
from jax.experimental.pallas import tpu as pltpu
from jax.sharding import PartitionSpec as P

MESH = pl.DeviceIdType.MESH
f32 = jnp.float32
bf16 = jnp.bfloat16
NT = (((1,), (1,)), ((), ()))

N_LEAF = 128
LEAVES = 16
LEAF = 256
RANK = 64
COLS = 16
NEAR = 8
FAR = 4
CUT = 4
SRC = NEAR + 1
SCALE = 5.0 * 1.4426950408889634
WEIGHT = 0.0625
TINY = 1e-30
BASE = (0, 16, 24, 28)
STRIP = 32


def split(x):
    high = x.astype(bf16)
    return high, (x - high.astype(f32)).astype(bf16)


def stacked(x):
    return jnp.concatenate(split(x), 0)


def fold(d):
    half = d.shape[0] // 2
    return d[:half] + d[half:]


def turned(x):
    return pltpu.roll(x, RANK, 1)


def low_lanes(shape):
    return lax.broadcasted_iota(jnp.int32, shape, 1) < RANK


def pick(a, b):
    return jnp.where(low_lanes(a.shape), a, b)


def both(r):
    return r + turned(r)


def halves(wide):
    high = wide.astype(bf16).astype(f32)
    return jnp.concatenate([high, wide - high], 1).astype(bf16)


def dot(a, b):
    return jnp.dot(a, b, preferred_element_type=f32)


def dot_t(a, b):
    return lax.dot_general(a, b, NT, preferred_element_type=f32)


def kernel(
    near_ref, far_ref, coarse_ref, vec_in, pts_in, bas_in, tra_in, cou_in,
    out_ref,
    vec, pts, bas, tra, cou, hv, hp, vh, rows, cols, buf_a, buf_b,
    ups, gath, tt, cc, bb, near_out,
    loc, hs, hr, us, ur, zs, zr, ys, yr, cs, cr,
):
    me = lax.axis_index("leaf")
    zi, yi, ci = me // 16, lax.rem(me // 2, 8), lax.rem(me, 2)
    left = lax.rem(me + N_LEAF - 1, N_LEAF)
    right = lax.rem(me + 1, N_LEAF)
    sibling = me + 1 - 2 * ci

    def z_peer(k):
        return lax.rem(zi + k, 8) * 16 + yi * 2 + ci

    def y_peer(k):
        return zi * 16 + lax.rem(yi + k, 8) * 2 + ci

    barrier = pltpu.get_barrier_semaphore()
    for peer in [left, right] + [z_peer(k) for k in range(1, 8)] + [y_peer(k) for k in range(1, 8)]:
        pl.semaphore_signal(barrier, inc=1, device_id={"leaf": peer}, device_id_type=MESH)

    locals_ = [
        pltpu.make_async_copy(src, dst, loc.at[i])
        for i, (src, dst) in enumerate(
            [(tra_in, tra), (cou_in, cou), (vec_in, vec), (bas_in, bas), (pts_in, pts)]
        )
    ]
    for copy in locals_:
        copy.start()

    def remote(src, dst, send, recv, peer):
        return pltpu.make_async_remote_copy(
            src_ref=src, dst_ref=dst, send_sem=send, recv_sem=recv,
            device_id={"leaf": peer}, device_id_type=MESH,
        )

    halo = [
        remote(vec_in, hv.at[0], hs.at[0], hr.at[0], right),
        remote(vec_in, hv.at[1], hs.at[1], hr.at[1], left),
        remote(pts_in, hp.at[0], hs.at[2], hr.at[2], right),
        remote(pts_in, hp.at[1], hs.at[3], hr.at[3], left),
    ]
    up_halo = [
        remote(ups.at[1], ups.at[0], us.at[0], ur.at[0], right),
        remote(ups.at[1], ups.at[2], us.at[1], ur.at[1], left),
    ]

    def z_copy(k):
        block = gath.at[zi, yi, ci]
        return remote(block, block, zs.at[k], zr.at[k], z_peer(k))

    def y_copy(k):
        block = gath.at[:, yi, ci]
        return remote(block, block, ys.at[k], yr.at[k], y_peer(k))

    half = gath.at[:, :, ci]
    c_copy = remote(half, half, cs, cr, sibling)

    locals_[0].wait()
    for k in range(6):
        for c in range(2):
            tt[k, c * RANK:(c + 1) * RANK, :] = halves(tra[k, c])

    pl.semaphore_wait(barrier, 16)
    for copy in halo:
        copy.start()

    locals_[2].wait()
    locals_[3].wait()
    level = []
    for leaf in range(LEAVES):
        s = stacked(vec[:, leaf * LEAF:(leaf + 1) * LEAF])
        vh[LEAVES + leaf] = jnp.concatenate([s, s], 1)
        b = stacked(bas[leaf])
        bb[leaf] = b
        level.append(both(fold(dot_t(s, b))))
    for k in range(CUT + 1):
        for n, u in enumerate(level):
            packed = pick(u[:8], u[8:])
            if k < CUT:
                ups[1, BASE[k] + n] = packed
            else:
                gath[zi, yi, ci] = packed
        if k < CUT:
            lhs = jnp.concatenate(
                [pick(level[2 * n], level[2 * n + 1]) for n in range(len(level) // 2)], 0
            )
            u = both(fold(dot(stacked(lhs), tt[k])))
            level = [u[n * COLS:(n + 1) * COLS] for n in range(len(level) // 2)]
    for k in range(1, 8):
        z_copy(k).start()
    for copy in up_halo:
        copy.start()

    locals_[1].wait()
    for k in range(7):
        for s in range(FAR):
            cc[k, s * RANK:(s + 1) * RANK, :] = halves(cou[k, s])

    def place(m, p):
        x = jnp.broadcast_to(p[0:1, :] * SCALE, (8, LEAF))
        y = jnp.broadcast_to(p[1:2, :] * SCALE, (8, LEAF))
        first = lax.broadcasted_iota(jnp.int32, (8, LEAF), 0) == 0
        cols[m, :, 0:8] = jnp.where(first, x, y).T
        return x, y

    locals_[4].wait()

    def own(i, _):
        at = pl.ds(pl.multiple_of(i * LEAF, LEAF), LEAF)
        x, y = place(LEAVES + i, pts[:, at])
        rows[i, 0] = x
        rows[i, 1] = y
        return 0

    lax.fori_loop(0, LEAVES, own, 0)
    for copy in halo:
        copy.wait_recv()

    def others(i, _):
        at = pl.ds(pl.multiple_of(i * LEAF, LEAF), LEAF)
        for side in range(2):
            m = 2 * LEAVES * side + i
            place(m, hp[side, :, at])
            s = stacked(hv[side, :, at])
            vh[m] = jnp.concatenate([s, s], 1)
        return 0

    lax.fori_loop(0, LEAVES, others, 0)

    first_leaf = (me - 1) * LEAVES

    def sources(t):
        return [LEAVES + t] + [
            jnp.clip(near_ref[j, t] - first_leaf, 0, 3 * LEAVES - 1) for j in range(NEAR)
        ]

    def weigh(t, buf):
        x = jnp.concatenate([rows[t, 0]] * (STRIP // 8), 0)
        y = jnp.concatenate([rows[t, 1]] * (STRIP // 8), 0)
        count = 0
        for j, m in enumerate(sources(t)):
            for r in range(0, LEAF, STRIP):
                sx = jnp.broadcast_to(cols[m, r:r + STRIP, 0:1], (STRIP, LEAF))
                sy = jnp.broadcast_to(cols[m, r:r + STRIP, 1:2], (STRIP, LEAF))
                dx, dy = sx - x, sy - y
                d2 = dx * dx + dy * dy
                if count % 4 < 3:
                    dist = pl.reciprocal(lax.rsqrt(d2), approx=True)
                else:
                    d2 = jnp.maximum(d2, TINY)
                    dist = d2 * lax.rsqrt(d2)
                count += 1
                high, low = split(jnp.exp2(-dist))
                at = j * 2 * LEAF + r
                buf[at:at + STRIP, :] = high
                buf[at + LEAF:at + LEAF + STRIP, :] = low

    def apply(t, buf):
        lhs = jnp.concatenate([vh[m] for m in sources(t)], 1)
        near_out[t] = fold(dot(lhs, buf[...])) * WEIGHT

    weigh(0, buf_a)

    def pair(i, _):
        @pl.when(i == 1)
        def _():
            for k in range(1, 8):
                z_copy(k).wait_recv()
            for k in range(1, 8):
                y_copy(k).start()

        @pl.when(i == 4)
        def _():
            for k in range(1, 8):
                y_copy(k).wait_recv()
            c_copy.start()

        apply(2 * i, buf_a)
        weigh(2 * i + 1, buf_b)
        apply(2 * i + 1, buf_b)
        weigh(2 * i + 2, buf_a)
        return 0

    lax.fori_loop(0, LEAVES // 2 - 1, pair, 0)

    for copy in up_halo:
        copy.wait_recv()
    c_copy.wait_recv()

    apply(LEAVES - 2, buf_a)
    weigh(LEAVES - 1, buf_b)
    apply(LEAVES - 1, buf_b)

    def four(xs):
        rs = [turned(x) for x in xs]
        return jnp.concatenate(
            [
                jnp.concatenate([pick(xs[s], rs[s + 1]), pick(rs[s], xs[s + 1])], 0)
                for s in (0, 2)
            ],
            1,
        )

    def cut_node(n):
        return gath[n // 16, lax.rem(n // 2, 8), lax.rem(n, 2)]

    def couple(lhs, k):
        return both(fold(dot(stacked(lhs), cc[k])))

    far = []
    for k in range(CUT):
        span = LEAVES >> k
        base = (me - 1) * span
        blocks = []
        for n in range(span):
            xs = []
            for s in range(FAR):
                at = jnp.clip(far_ref[k, s, n] - base, 0, 3 * span - 1)
                xs.append(ups[at // span, BASE[k] + lax.rem(at, span)])
            blocks.append(four(xs))
        far.append(couple(jnp.concatenate(blocks, 0), k))

    far_4 = couple(four([cut_node(coarse_ref[0, s, me]) for s in range(FAR)]), 4)

    def joined(n):
        a, b = cut_node(2 * n), cut_node(2 * n + 1)
        return jnp.concatenate([pick(a, turned(b)), pick(turned(a), b)], 0)

    mid, top = me // 2, me // 4
    blocks = [joined(coarse_ref[1, s, mid]) for s in range(FAR)]
    for s in range(FAR):
        n = coarse_ref[2, s, top]
        blocks += [joined(2 * n), joined(2 * n + 1)]
    u = both(fold(dot(stacked(jnp.concatenate(blocks, 0)), tt[4])))
    u = [u[n * COLS:(n + 1) * COLS] for n in range(12)]
    far_5 = couple(jnp.concatenate([pick(u[0], u[1]), pick(u[2], u[3])], 1), 5)
    lhs = jnp.concatenate([pick(u[4 + 2 * s], u[5 + 2 * s]) for s in range(FAR)], 0)
    u = both(fold(dot(stacked(lhs), tt[5])))
    u = [u[n * COLS:(n + 1) * COLS] for n in range(4)]
    down = couple(jnp.concatenate([pick(u[0], u[1]), pick(u[2], u[3])], 1), 6)

    def children(d, k):
        r = fold(dot_t(stacked(d), tt[k]))
        t = turned(r)
        return pick(r, t), pick(t, r)

    for k, node, here in ((5, mid, far_5), (4, me, far_4)):
        a, b = children(down, k)
        down = here + jnp.where(lax.rem(node, 2) == 0, a, b)
    for k in range(CUT - 1, -1, -1):
        a, b = children(down, k)
        parts = []
        for n in range(a.shape[0] // COLS):
            at = slice(n * COLS, (n + 1) * COLS)
            parts += [a[at], b[at]]
        down = far[k] + jnp.concatenate(parts, 0)

    for leaf in range(LEAVES):
        d = stacked(down[leaf * COLS:(leaf + 1) * COLS])
        out_ref[:, leaf * LEAF:(leaf + 1) * LEAF] = near_out[leaf] + fold(dot(d, bb[leaf]))

    for copy in halo + up_halo + [c_copy]:
        copy.wait_send()
    for k in range(1, 8):
        z_copy(k).wait_send()
        y_copy(k).wait_send()


def local(vectors, points, bases, transfer, coupling, near_lists, far_lists, coarse_lists):
    smem = pl.BlockSpec(memory_space=pltpu.SMEM)
    anywhere = pl.BlockSpec(memory_space=pl.ANY)
    vmem = pltpu.VMEM
    dma = pltpu.SemaphoreType.DMA
    return pl.pallas_call(
        kernel,
        out_shape=jax.ShapeDtypeStruct(vectors.shape, f32),
        in_specs=[smem] * 3 + [anywhere] * 5,
        out_specs=pl.BlockSpec(memory_space=vmem),
        scratch_shapes=[
            vmem((COLS, LEAVES * LEAF), f32),
            vmem((2, LEAVES * LEAF), f32),
            vmem((LEAVES, RANK, LEAF), f32),
            vmem((6, 2, RANK, RANK), f32),
            vmem((7, FAR, RANK, RANK), f32),
            vmem((2, COLS, LEAVES * LEAF), f32),
            vmem((2, 2, LEAVES * LEAF), f32),
            vmem((3 * LEAVES, 2 * COLS, 2 * LEAF), bf16),
            vmem((LEAVES, 2, 8, LEAF), f32),
            vmem((3 * LEAVES, LEAF, 128), f32),
            vmem((SRC * 2 * LEAF, LEAF), bf16),
            vmem((SRC * 2 * LEAF, LEAF), bf16),
            vmem((3, 30, 8, 128), f32),
            vmem((8, 8, 2, 8, 128), f32),
            vmem((6, 2 * RANK, 2 * RANK), bf16),
            vmem((7, FAR * RANK, 2 * RANK), bf16),
            vmem((LEAVES, 2 * RANK, LEAF), bf16),
            vmem((LEAVES, COLS, LEAF), f32),
            dma((5,)), dma((4,)), dma((4,)), dma((2,)), dma((2,)),
            dma((8,)), dma((8,)), dma((8,)), dma((8,)), dma, dma,
        ],
        compiler_params=pltpu.CompilerParams(
            collective_id=0, has_side_effects=True, vmem_limit_bytes=50 * 2**20
        ),
    )(
        near_lists.T,
        far_lists.transpose(0, 2, 1),
        coarse_lists.transpose(0, 2, 1),
        vectors,
        points,
        bases.transpose(0, 2, 1),
        transfer,
        coupling,
    )


def solution(mesh):
    in_specs = (
        P("vec", "leaf"),
        P(None, "leaf"),
        P("leaf", None, None),
        P(),
        P(),
        P("leaf", None),
        P(None, "leaf", None),
        P(),
    )
    return jax.shard_map(
        local, mesh=mesh, in_specs=in_specs, out_specs=P("vec", "leaf"), check_vma=False
    )
```

```python
import functools

import jax
import jax.numpy as jnp
from jax import lax
from jax.experimental import pallas as pl
from jax.experimental.pallas import tpu as pltpu
from jax.sharding import PartitionSpec as P

MESH = pl.DeviceIdType.MESH
f32 = jnp.float32
bf16 = jnp.bfloat16
NT = (((1,), (1,)), ((), ()))

N_LEAF = 128
LEAVES = 16
LEAF = 256
RANK = 64
COLS = 16
NEAR = 8
FAR = 4
CUT = 4
SRC = NEAR + 1
SCALE = 5.0 * 1.4426950408889634
WEIGHT = 0.0625
TINY = 1e-30
BASE = (0, 16, 24, 28)
STRIP = 32


def split(x):
    high = x.astype(bf16)
    return high, (x - high.astype(f32)).astype(bf16)


def stacked(x):
    return jnp.concatenate(split(x), 0)


def fold(d):
    half = d.shape[0] // 2
    return d[:half] + d[half:]


def turned(x):
    return pltpu.roll(x, RANK, 1)


def low_lanes(shape):
    return lax.broadcasted_iota(jnp.int32, shape, 1) < RANK


def pick(a, b):
    return jnp.where(low_lanes(a.shape), a, b)


def both(r):
    return r + turned(r)


def halves(wide):
    high = wide.astype(bf16).astype(f32)
    return jnp.concatenate([high, wide - high], 1).astype(bf16)


def dot(a, b):
    return jnp.dot(a, b, preferred_element_type=f32)


def dot_t(a, b):
    return lax.dot_general(a, b, NT, preferred_element_type=f32)


def kernel(
    near_ref, far_ref, coarse_ref, vec_in, pts_in, bas_in, tra_in, cou_in,
    out_ref,
    vec, pts, bas, tra, cou, hv, hp, vh, rows, cols, buf_a, buf_b,
    ups, gath, tt, cc, bb, near_out,
    loc, hs, hr, us, ur, zs, zr, ys, yr, cs, cr, chain,
):
    me = lax.axis_index("leaf")
    zi, yi, ci = me // 16, lax.rem(me // 2, 8), lax.rem(me, 2)
    left, right = me - 1, me + 1
    sibling = me + 1 - 2 * ci

    def y_peer(k):
        return zi * 16 + lax.rem(yi + k, 8) * 2 + ci

    def signal(sem, peer):
        pl.semaphore_signal(sem, inc=1, device_id={"leaf": peer}, device_id_type=MESH)

    beside = [
        (me > 0, me - 1),
        (me < N_LEAF - 1, me + 1),
        (zi > 0, me - 16),
        (zi < 7, me + 16),
    ]
    barrier = pltpu.get_barrier_semaphore()
    for k in range(1, 8):
        signal(barrier, y_peer(k))
    greeted = 7
    for there, peer in beside:
        greeted += there.astype(jnp.int32)
        pl.when(there)(functools.partial(signal, barrier, peer))

    locals_ = [
        pltpu.make_async_copy(src, dst, loc.at[i])
        for i, (src, dst) in enumerate(
            [(tra_in, tra), (cou_in, cou), (vec_in, vec), (bas_in, bas), (pts_in, pts)]
        )
    ]
    for copy in locals_:
        copy.start()

    def remote(src, dst, send, recv, peer):
        return pltpu.make_async_remote_copy(
            src_ref=src, dst_ref=dst, send_sem=send, recv_sem=recv,
            device_id={"leaf": peer}, device_id_type=MESH,
        )

    to_right = [
        remote(vec_in, hv.at[0], hs.at[0], hr.at[0], right),
        remote(pts_in, hp.at[0], hs.at[1], hr.at[1], right),
    ]
    to_left = [
        remote(vec_in, hv.at[1], hs.at[2], hr.at[2], left),
        remote(pts_in, hp.at[1], hs.at[3], hr.at[3], left),
    ]
    up_right = [remote(ups.at[1], ups.at[0], us.at[0], ur.at[0], right)]
    up_left = [remote(ups.at[1], ups.at[2], us.at[1], ur.at[1], left)]

    def run(step, copies):
        for copy in copies:
            getattr(copy, step)()

    def send(rightward, leftward, step):
        pl.when(me < N_LEAF - 1)(functools.partial(run, step, rightward))
        pl.when(me > 0)(functools.partial(run, step, leftward))

    def receive(rightward, leftward):
        pl.when(me > 0)(functools.partial(run, "wait_recv", rightward))
        pl.when(me < N_LEAF - 1)(functools.partial(run, "wait_recv", leftward))

    def z_send(to, step):
        block = gath.at[zi, yi, ci]
        run(step, [remote(block, block, zs.at[to], zr.at[zi], to * 16 + yi * 2 + ci)])

    def z_receive(source):
        block = gath.at[source, yi, ci]
        run("wait_recv", [remote(block, block, zs.at[source], zr.at[source], source * 16 + yi * 2 + ci)])

    def lower(f, *args):
        for z in range(7):
            pl.when(z < zi)(functools.partial(f, z, *args))

    def higher(f, *args):
        for z in range(1, 8):
            pl.when(z > zi)(functools.partial(f, z, *args))

    def y_copy(k):
        block = gath.at[:, yi, ci]
        return remote(block, block, ys.at[k], yr.at[k], y_peer(k))

    half = gath.at[:, :, ci]
    c_copy = remote(half, half, cs, cr, sibling)

    locals_[0].wait()
    for k in range(6):
        for c in range(2):
            tt[k, c * RANK:(c + 1) * RANK, :] = halves(tra[k, c])

    pl.semaphore_wait(barrier, greeted)
    send(to_right, to_left, "start")

    @pl.when(zi > 0)
    def _():
        pl.semaphore_wait(chain, 1)

    pl.when(zi < 7)(functools.partial(signal, chain, me + 16))

    locals_[2].wait()
    locals_[3].wait()
    level = []
    for leaf in range(LEAVES):
        s = stacked(vec[:, leaf * LEAF:(leaf + 1) * LEAF])
        vh[LEAVES + leaf] = jnp.concatenate([s, s], 1)
        b = stacked(bas[leaf])
        bb[leaf] = b
        level.append(both(fold(dot_t(s, b))))
    for k in range(CUT + 1):
        for n, u in enumerate(level):
            packed = pick(u[:8], u[8:])
            if k < CUT:
                ups[1, BASE[k] + n] = packed
            else:
                gath[zi, yi, ci] = packed
        if k < CUT:
            lhs = jnp.concatenate(
                [pick(level[2 * n], level[2 * n + 1]) for n in range(len(level) // 2)], 0
            )
            u = both(fold(dot(stacked(lhs), tt[k])))
            level = [u[n * COLS:(n + 1) * COLS] for n in range(len(level) // 2)]
    lower(z_send, "start")
    send(up_right, up_left, "start")

    locals_[1].wait()
    for k in range(7):
        for s in range(FAR):
            cc[k, s * RANK:(s + 1) * RANK, :] = halves(cou[k, s])

    def place(m, p):
        x = jnp.broadcast_to(p[0:1, :] * SCALE, (8, LEAF))
        y = jnp.broadcast_to(p[1:2, :] * SCALE, (8, LEAF))
        first = lax.broadcasted_iota(jnp.int32, (8, LEAF), 0) == 0
        cols[m, :, 0:8] = jnp.where(first, x, y).T
        return x, y

    locals_[4].wait()

    def own(i, _):
        at = pl.ds(pl.multiple_of(i * LEAF, LEAF), LEAF)
        x, y = place(LEAVES + i, pts[:, at])
        rows[i, 0] = x
        rows[i, 1] = y
        return 0

    lax.fori_loop(0, LEAVES, own, 0)
    receive(to_right, to_left)

    def others(i, _):
        at = pl.ds(pl.multiple_of(i * LEAF, LEAF), LEAF)
        for side in range(2):
            m = 2 * LEAVES * side + i
            place(m, hp[side, :, at])
            s = stacked(hv[side, :, at])
            vh[m] = jnp.concatenate([s, s], 1)
        return 0

    lax.fori_loop(0, LEAVES, others, 0)

    first_leaf = (me - 1) * LEAVES

    def sources(t):
        return [LEAVES + t] + [
            jnp.clip(near_ref[j, t] - first_leaf, 0, 3 * LEAVES - 1) for j in range(NEAR)
        ]

    def weigh(t, buf):
        x = jnp.concatenate([rows[t, 0]] * (STRIP // 8), 0)
        y = jnp.concatenate([rows[t, 1]] * (STRIP // 8), 0)
        count = 0
        for j, m in enumerate(sources(t)):
            for r in range(0, LEAF, STRIP):
                sx = jnp.broadcast_to(cols[m, r:r + STRIP, 0:1], (STRIP, LEAF))
                sy = jnp.broadcast_to(cols[m, r:r + STRIP, 1:2], (STRIP, LEAF))
                dx, dy = sx - x, sy - y
                d2 = dx * dx + dy * dy
                if count % 4 < 3:
                    dist = pl.reciprocal(lax.rsqrt(d2), approx=True)
                else:
                    d2 = jnp.maximum(d2, TINY)
                    dist = d2 * lax.rsqrt(d2)
                count += 1
                high, low = split(jnp.exp2(-dist))
                at = j * 2 * LEAF + r
                buf[at:at + STRIP, :] = high
                buf[at + LEAF:at + LEAF + STRIP, :] = low

    def apply(t, buf):
        lhs = jnp.concatenate([vh[m] for m in sources(t)], 1)
        near_out[t] = fold(dot(lhs, buf[...])) * WEIGHT

    weigh(0, buf_a)

    def pair(i, _):
        @pl.when(i == 3)
        def _():
            higher(z_receive)
            higher(z_send, "start")

        @pl.when(i == 4)
        def _():
            lower(z_receive)
            for k in range(1, 8):
                y_copy(k).start()

        @pl.when(i == 6)
        def _():
            for k in range(1, 8):
                y_copy(k).wait_recv()
            c_copy.start()

        apply(2 * i, buf_a)
        weigh(2 * i + 1, buf_b)
        apply(2 * i + 1, buf_b)
        weigh(2 * i + 2, buf_a)
        return 0

    lax.fori_loop(0, LEAVES // 2 - 1, pair, 0)

    apply(LEAVES - 2, buf_a)
    weigh(LEAVES - 1, buf_b)

    receive(up_right, up_left)
    c_copy.wait_recv()
    apply(LEAVES - 1, buf_b)

    def four(xs):
        rs = [turned(x) for x in xs]
        return jnp.concatenate(
            [
                jnp.concatenate([pick(xs[s], rs[s + 1]), pick(rs[s], xs[s + 1])], 0)
                for s in (0, 2)
            ],
            1,
        )

    def cut_node(n):
        return gath[n // 16, lax.rem(n // 2, 8), lax.rem(n, 2)]

    def couple(lhs, k):
        return both(fold(dot(stacked(lhs), cc[k])))

    far = []
    for k in range(CUT):
        span = LEAVES >> k
        base = (me - 1) * span
        blocks = []
        for n in range(span):
            xs = []
            for s in range(FAR):
                at = jnp.clip(far_ref[k, s, n] - base, 0, 3 * span - 1)
                xs.append(ups[at // span, BASE[k] + lax.rem(at, span)])
            blocks.append(four(xs))
        far.append(couple(jnp.concatenate(blocks, 0), k))

    far_4 = couple(four([cut_node(coarse_ref[0, s, me]) for s in range(FAR)]), 4)

    def joined(n):
        a, b = cut_node(2 * n), cut_node(2 * n + 1)
        return jnp.concatenate([pick(a, turned(b)), pick(turned(a), b)], 0)

    mid, top = me // 2, me // 4
    blocks = [joined(coarse_ref[1, s, mid]) for s in range(FAR)]
    for s in range(FAR):
        n = coarse_ref[2, s, top]
        blocks += [joined(2 * n), joined(2 * n + 1)]
    u = both(fold(dot(stacked(jnp.concatenate(blocks, 0)), tt[4])))
    u = [u[n * COLS:(n + 1) * COLS] for n in range(12)]
    far_5 = couple(jnp.concatenate([pick(u[0], u[1]), pick(u[2], u[3])], 1), 5)
    lhs = jnp.concatenate([pick(u[4 + 2 * s], u[5 + 2 * s]) for s in range(FAR)], 0)
    u = both(fold(dot(stacked(lhs), tt[5])))
    u = [u[n * COLS:(n + 1) * COLS] for n in range(4)]
    down = couple(jnp.concatenate([pick(u[0], u[1]), pick(u[2], u[3])], 1), 6)

    def children(d, k):
        r = fold(dot_t(stacked(d), tt[k]))
        t = turned(r)
        return pick(r, t), pick(t, r)

    for k, node, here in ((5, mid, far_5), (4, me, far_4)):
        a, b = children(down, k)
        down = here + jnp.where(lax.rem(node, 2) == 0, a, b)
    for k in range(CUT - 1, -1, -1):
        a, b = children(down, k)
        parts = []
        for n in range(a.shape[0] // COLS):
            at = slice(n * COLS, (n + 1) * COLS)
            parts += [a[at], b[at]]
        down = far[k] + jnp.concatenate(parts, 0)

    for leaf in range(LEAVES):
        d = stacked(down[leaf * COLS:(leaf + 1) * COLS])
        out_ref[:, leaf * LEAF:(leaf + 1) * LEAF] = near_out[leaf] + fold(dot(d, bb[leaf]))

    send(to_right, to_left, "wait_send")
    send(up_right, up_left, "wait_send")
    lower(z_send, "wait_send")
    higher(z_send, "wait_send")
    for k in range(1, 8):
        y_copy(k).wait_send()
    c_copy.wait_send()


def local(vectors, points, bases, transfer, coupling, near_lists, far_lists, coarse_lists):
    smem = pl.BlockSpec(memory_space=pltpu.SMEM)
    anywhere = pl.BlockSpec(memory_space=pl.ANY)
    vmem = pltpu.VMEM
    dma = pltpu.SemaphoreType.DMA
    return pl.pallas_call(
        kernel,
        out_shape=jax.ShapeDtypeStruct(vectors.shape, f32),
        in_specs=[smem] * 3 + [anywhere] * 5,
        out_specs=pl.BlockSpec(memory_space=vmem),
        scratch_shapes=[
            vmem((COLS, LEAVES * LEAF), f32),
            vmem((2, LEAVES * LEAF), f32),
            vmem((LEAVES, RANK, LEAF), f32),
            vmem((6, 2, RANK, RANK), f32),
            vmem((7, FAR, RANK, RANK), f32),
            vmem((2, COLS, LEAVES * LEAF), f32),
            vmem((2, 2, LEAVES * LEAF), f32),
            vmem((3 * LEAVES, 2 * COLS, 2 * LEAF), bf16),
            vmem((LEAVES, 2, 8, LEAF), f32),
            vmem((3 * LEAVES, LEAF, 128), f32),
            vmem((SRC * 2 * LEAF, LEAF), bf16),
            vmem((SRC * 2 * LEAF, LEAF), bf16),
            vmem((3, 30, 8, 128), f32),
            vmem((8, 8, 2, 8, 128), f32),
            vmem((6, 2 * RANK, 2 * RANK), bf16),
            vmem((7, FAR * RANK, 2 * RANK), bf16),
            vmem((LEAVES, 2 * RANK, LEAF), bf16),
            vmem((LEAVES, COLS, LEAF), f32),
            dma((5,)), dma((4,)), dma((4,)), dma((2,)), dma((2,)),
            dma((8,)), dma((8,)), dma((8,)), dma((8,)), dma, dma,
            pltpu.SemaphoreType.REGULAR,
        ],
        compiler_params=pltpu.CompilerParams(
            collective_id=0, has_side_effects=True, vmem_limit_bytes=64 * 2**20 - 2**16
        ),
    )(
        near_lists.T,
        far_lists.transpose(0, 2, 1),
        coarse_lists.transpose(0, 2, 1),
        vectors,
        points,
        bases.transpose(0, 2, 1),
        transfer,
        coupling,
    )


def solution(mesh):
    in_specs = (
        P("vec", "leaf"),
        P(None, "leaf"),
        P("leaf", None, None),
        P(),
        P(),
        P("leaf", None),
        P(None, "leaf", None),
        P(),
    )
    return jax.shard_map(
        local, mesh=mesh, in_specs=in_specs, out_specs=P("vec", "leaf"), check_vma=False
    )
```

```python
import functools

import jax
import jax.numpy as jnp
from jax import lax
from jax.experimental import pallas as pl
from jax.experimental.pallas import tpu as pltpu
from jax.sharding import PartitionSpec as P

MESH = pl.DeviceIdType.MESH
f32 = jnp.float32
bf16 = jnp.bfloat16
NT = (((1,), (1,)), ((), ()))

N_LEAF = 128
LEAVES = 16
LEAF = 256
RANK = 64
COLS = 16
NEAR = 8
FAR = 4
CUT = 4
SCALE = 5.0 * 1.4426950408889634
WEIGHT = 0.0625
TINY = 1e-30
BASE = (0, 16, 24, 28)
STRIP = 32


def split(x):
    high = x.astype(bf16)
    return high, (x - high.astype(f32)).astype(bf16)


def stacked(x):
    return jnp.concatenate(split(x), 0)


def fold(d):
    half = d.shape[0] // 2
    return d[:half] + d[half:]


def turned(x):
    return pltpu.roll(x, RANK, 1)


def low_lanes(shape):
    return lax.broadcasted_iota(jnp.int32, shape, 1) < RANK


def pick(a, b):
    return jnp.where(low_lanes(a.shape), a, b)


def both(r):
    return r + turned(r)


def halves(wide):
    high = wide.astype(bf16).astype(f32)
    return jnp.concatenate([high, wide - high], 1).astype(bf16)


def dot(a, b):
    return jnp.dot(a, b, preferred_element_type=f32)


def dot_t(a, b):
    return lax.dot_general(a, b, NT, preferred_element_type=f32)


def kernel(
    near_in, far_in, coarse_in, vec_in, pts_in, bas_in, tra_in, cou_in,
    out_ref,
    near_ref, far_ref, coarse_ref,
    vec, pts, bas, tra, cou, hv, hp, vh, rows, cols, buf_a, buf_b,
    ups, gath, tt, cc, bb, near_out,
    loc, hs, hr, us, ur, zs, zr, ys, yr, cs, cr, chain,
):
    me = lax.axis_index("leaf")
    zi, yi, ci = me // 16, lax.rem(me // 2, 8), lax.rem(me, 2)
    left, right = me - 1, me + 1
    sibling = me + 1 - 2 * ci

    def y_peer(k):
        return zi * 16 + lax.rem(yi + k, 8) * 2 + ci

    def signal(sem, peer):
        pl.semaphore_signal(sem, inc=1, device_id={"leaf": peer}, device_id_type=MESH)

    beside = [
        (me > 0, me - 1),
        (me < N_LEAF - 1, me + 1),
        (zi > 0, me - 16),
        (zi < 7, me + 16),
    ]
    barrier = pltpu.get_barrier_semaphore()
    for k in range(1, 8):
        signal(barrier, y_peer(k))
    greeted = 7
    for there, peer in beside:
        greeted += there.astype(jnp.int32)
        pl.when(there)(functools.partial(signal, barrier, peer))

    locals_ = [
        pltpu.make_async_copy(src, dst, loc.at[i])
        for i, (src, dst) in enumerate(
            [
                (tra_in, tra), (cou_in, cou), (vec_in, vec), (bas_in, bas), (pts_in, pts),
                (near_in, near_ref), (far_in, far_ref), (coarse_in, coarse_ref),
            ]
        )
    ]
    for copy in locals_:
        copy.start()

    def remote(src, dst, send, recv, peer):
        return pltpu.make_async_remote_copy(
            src_ref=src, dst_ref=dst, send_sem=send, recv_sem=recv,
            device_id={"leaf": peer}, device_id_type=MESH,
        )

    to_right = [
        remote(vec_in, hv.at[0], hs.at[0], hr.at[0], right),
        remote(pts_in, hp.at[0], hs.at[1], hr.at[1], right),
    ]
    to_left = [
        remote(vec_in, hv.at[1], hs.at[2], hr.at[2], left),
        remote(pts_in, hp.at[1], hs.at[3], hr.at[3], left),
    ]
    up_right = [remote(ups.at[1], ups.at[0], us.at[0], ur.at[0], right)]
    up_left = [remote(ups.at[1], ups.at[2], us.at[1], ur.at[1], left)]

    def run(step, copies):
        for copy in copies:
            getattr(copy, step)()

    def send(rightward, leftward, step):
        pl.when(me < N_LEAF - 1)(functools.partial(run, step, rightward))
        pl.when(me > 0)(functools.partial(run, step, leftward))

    def receive(rightward, leftward):
        pl.when(me > 0)(functools.partial(run, "wait_recv", rightward))
        pl.when(me < N_LEAF - 1)(functools.partial(run, "wait_recv", leftward))

    def z_send(to, step):
        block = gath.at[zi, ci]
        run(step, [remote(block, block, zs.at[to], zr.at[zi], to * 16 + yi * 2 + ci)])

    def z_receive(source):
        block = gath.at[source, ci]
        run("wait_recv", [remote(block, block, zs.at[source], zr.at[source], source * 16 + yi * 2 + ci)])

    def lower(f, *args):
        for z in range(7):
            pl.when(z < zi)(functools.partial(f, z, *args))

    def higher(f, *args):
        for z in range(1, 8):
            pl.when(z > zi)(functools.partial(f, z, *args))

    def y_copy(k):
        block = gath.at[zi, ci, yi]
        return remote(block, block, ys.at[k], yr.at[k], y_peer(k))

    def y_receive(k):
        block = gath.at[zi, ci, lax.rem(yi + 8 - k, 8)]
        run("wait_recv", [remote(block, block, ys.at[k], yr.at[k], y_peer(8 - k))])

    def c_send(z, step):
        block = gath.at[z, ci]
        run(step, [remote(block, block, cs.at[z], cr.at[z], sibling)])

    def c_receive(z):
        block = gath.at[z, 1 - ci]
        run("wait_recv", [remote(block, block, cs.at[z], cr.at[z], sibling)])

    locals_[0].wait()
    for k in range(6):
        for c in range(2):
            tt[k, c * RANK:(c + 1) * RANK, :] = halves(tra[k, c])

    pl.semaphore_wait(barrier, greeted)
    send(to_right, to_left, "start")

    @pl.when(zi > 0)
    def _():
        pl.semaphore_wait(chain, 1)

    pl.when(zi < 7)(functools.partial(signal, chain, me + 16))

    locals_[2].wait()
    locals_[3].wait()
    level = []
    for leaf in range(LEAVES):
        s = stacked(vec[:, leaf * LEAF:(leaf + 1) * LEAF])
        vh[LEAVES + leaf] = jnp.concatenate([s, s], 1)
        b = stacked(bas[leaf])
        bb[leaf] = b
        level.append(both(fold(dot_t(s, b))))
    for k in range(CUT + 1):
        for n, u in enumerate(level):
            packed = pick(u[:8], u[8:])
            if k < CUT:
                ups[1, BASE[k] + n] = packed
            else:
                gath[zi, ci, yi] = packed
        if k < CUT:
            lhs = jnp.concatenate(
                [pick(level[2 * n], level[2 * n + 1]) for n in range(len(level) // 2)], 0
            )
            u = both(fold(dot(stacked(lhs), tt[k])))
            level = [u[n * COLS:(n + 1) * COLS] for n in range(len(level) // 2)]
    for k in range(1, 8):
        y_copy(k).start()
    send(up_right, up_left, "start")

    locals_[1].wait()
    for k in range(7):
        for s in range(FAR):
            cc[k, s * RANK:(s + 1) * RANK, :] = halves(cou[k, s])

    def place(m, p):
        x = jnp.broadcast_to(p[0:1, :] * SCALE, (8, LEAF))
        y = jnp.broadcast_to(p[1:2, :] * SCALE, (8, LEAF))
        first = lax.broadcasted_iota(jnp.int32, (8, LEAF), 0) == 0
        cols[m, :, 0:8] = jnp.where(first, x, y).T
        return x, y

    def weights(x, y, m, put):
        x = jnp.concatenate([x] * (STRIP // 8), 0)
        y = jnp.concatenate([y] * (STRIP // 8), 0)
        for r in range(0, LEAF, STRIP):
            sx = jnp.broadcast_to(cols[m, r:r + STRIP, 0:1], (STRIP, LEAF))
            sy = jnp.broadcast_to(cols[m, r:r + STRIP, 1:2], (STRIP, LEAF))
            dx, dy = sx - x, sy - y
            d2 = dx * dx + dy * dy
            if (r // STRIP) % 4 < 3:
                dist = pl.reciprocal(lax.rsqrt(d2), approx=True)
            else:
                d2 = jnp.maximum(d2, TINY)
                dist = d2 * lax.rsqrt(d2)
            put(r, *split(jnp.exp2(-dist)))

    locals_[4].wait()

    def own(i, _):
        for n in range(4):
            t = i * 4 + n
            x, y = place(LEAVES + t, pts[:, pl.ds(pl.multiple_of(t * LEAF, LEAF), LEAF)])
            rows[t, 0] = x
            rows[t, 1] = y
            highs, lows = [], []

            def put(r, high, low):
                highs.append(high)
                lows.append(low)

            weights(x, y, LEAVES + t, put)
            near_out[t] = fold(dot(vh[LEAVES + t], jnp.concatenate(highs + lows, 0)))
        return 0

    lax.fori_loop(0, LEAVES // 4, own, 0)
    for k in range(1, 8):
        y_receive(k)
    lower(z_send, "start")
    c_send(zi, "start")
    for copy in locals_[5:]:
        copy.wait()
    receive(to_right, to_left)

    def others(i, _):
        for n in range(4):
            t = i * 4 + n
            at = pl.ds(pl.multiple_of(t * LEAF, LEAF), LEAF)
            for side in range(2):
                m = 2 * LEAVES * side + t
                place(m, hp[side, :, at])
                s = stacked(hv[side, :, at])
                vh[m] = jnp.concatenate([s, s], 1)
        return 0

    lax.fori_loop(0, LEAVES // 4, others, 0)

    first_leaf = (me - 1) * LEAVES

    def sources(t):
        return [
            jnp.clip(near_ref[j, t] - first_leaf, 0, 3 * LEAVES - 1) for j in range(NEAR)
        ]

    def weigh(t, buf):
        for j, m in enumerate(sources(t)):
            def put(r, high, low, at=j * 2 * LEAF):
                buf[at + r:at + r + STRIP, :] = high
                buf[at + LEAF + r:at + LEAF + r + STRIP, :] = low

            weights(rows[t, 0], rows[t, 1], m, put)

    def apply(t, buf):
        lhs = jnp.concatenate([vh[m] for m in sources(t)], 1)
        near_out[t] = (near_out[t] + fold(dot(lhs, buf[...]))) * WEIGHT

    weigh(0, buf_a)

    def pair(i, _):
        @pl.when(i == 3)
        def _():
            higher(z_receive)
            higher(z_send, "start")
            higher(c_send, "start")

        @pl.when(i == 5)
        def _():
            lower(z_receive)
            lower(c_send, "start")

        apply(2 * i, buf_a)
        weigh(2 * i + 1, buf_b)
        apply(2 * i + 1, buf_b)
        weigh(2 * i + 2, buf_a)
        return 0

    lax.fori_loop(0, LEAVES // 2 - 1, pair, 0)

    receive(up_right, up_left)
    for z in range(8):
        c_receive(z)
    apply(LEAVES - 2, buf_a)
    weigh(LEAVES - 1, buf_b)

    def four(xs):
        rs = [turned(x) for x in xs]
        return jnp.concatenate(
            [
                jnp.concatenate([pick(xs[s], rs[s + 1]), pick(rs[s], xs[s + 1])], 0)
                for s in (0, 2)
            ],
            1,
        )

    def cut_node(n):
        return gath[n // 16, lax.rem(n, 2), lax.rem(n // 2, 8)]

    def couple(lhs, k):
        return both(fold(dot(stacked(lhs), cc[k])))

    far = []
    for k in range(CUT):
        span = LEAVES >> k
        base = (me - 1) * span
        blocks = []
        for n in range(span):
            xs = []
            for s in range(FAR):
                at = jnp.clip(far_ref[k, s, n] - base, 0, 3 * span - 1)
                xs.append(ups[at // span, BASE[k] + lax.rem(at, span)])
            blocks.append(four(xs))
        far.append(couple(jnp.concatenate(blocks, 0), k))

    far_4 = couple(four([cut_node(coarse_ref[0, s, me]) for s in range(FAR)]), 4)

    def joined(n):
        a, b = cut_node(2 * n), cut_node(2 * n + 1)
        return jnp.concatenate([pick(a, turned(b)), pick(turned(a), b)], 0)

    mid, top = me // 2, me // 4
    blocks = [joined(coarse_ref[1, s, mid]) for s in range(FAR)]
    for s in range(FAR):
        n = coarse_ref[2, s, top]
        blocks += [joined(2 * n), joined(2 * n + 1)]
    u = both(fold(dot(stacked(jnp.concatenate(blocks, 0)), tt[4])))
    u = [u[n * COLS:(n + 1) * COLS] for n in range(12)]
    far_5 = couple(jnp.concatenate([pick(u[0], u[1]), pick(u[2], u[3])], 1), 5)
    lhs = jnp.concatenate([pick(u[4 + 2 * s], u[5 + 2 * s]) for s in range(FAR)], 0)
    u = both(fold(dot(stacked(lhs), tt[5])))
    u = [u[n * COLS:(n + 1) * COLS] for n in range(4)]
    down = couple(jnp.concatenate([pick(u[0], u[1]), pick(u[2], u[3])], 1), 6)

    def children(d, k):
        r = fold(dot_t(stacked(d), tt[k]))
        t = turned(r)
        return pick(r, t), pick(t, r)

    for k, node, here in ((5, mid, far_5), (4, me, far_4)):
        a, b = children(down, k)
        down = here + jnp.where(lax.rem(node, 2) == 0, a, b)
    for k in range(CUT - 1, -1, -1):
        a, b = children(down, k)
        parts = []
        for n in range(a.shape[0] // COLS):
            at = slice(n * COLS, (n + 1) * COLS)
            parts += [a[at], b[at]]
        down = far[k] + jnp.concatenate(parts, 0)

    apply(LEAVES - 1, buf_b)
    for leaf in range(LEAVES):
        d = stacked(down[leaf * COLS:(leaf + 1) * COLS])
        out_ref[:, leaf * LEAF:(leaf + 1) * LEAF] = near_out[leaf] + fold(dot(d, bb[leaf]))

    send(to_right, to_left, "wait_send")
    send(up_right, up_left, "wait_send")
    lower(z_send, "wait_send")
    higher(z_send, "wait_send")
    for k in range(1, 8):
        y_copy(k).wait_send()
    for z in range(8):
        c_send(z, "wait_send")


def local(vectors, points, bases, transfer, coupling, near_lists, far_lists, coarse_lists):
    outside = pl.BlockSpec(memory_space=pltpu.HBM)
    smem = pltpu.SMEM
    vmem = pltpu.VMEM
    dma = pltpu.SemaphoreType.DMA
    return pl.pallas_call(
        kernel,
        out_shape=jax.ShapeDtypeStruct(vectors.shape, f32),
        in_specs=[outside] * 8,
        out_specs=pl.BlockSpec(memory_space=vmem),
        scratch_shapes=[
            smem((NEAR, LEAVES), jnp.int32),
            smem((CUT, FAR, LEAVES), jnp.int32),
            smem((3, FAR, N_LEAF), jnp.int32),
            vmem((COLS, LEAVES * LEAF), f32),
            vmem((2, LEAVES * LEAF), f32),
            vmem((LEAVES, RANK, LEAF), f32),
            vmem((6, 2, RANK, RANK), f32),
            vmem((7, FAR, RANK, RANK), f32),
            vmem((2, COLS, LEAVES * LEAF), f32),
            vmem((2, 2, LEAVES * LEAF), f32),
            vmem((3 * LEAVES, 2 * COLS, 2 * LEAF), bf16),
            vmem((LEAVES, 2, 8, LEAF), f32),
            vmem((3 * LEAVES, LEAF, 128), f32),
            vmem((NEAR * 2 * LEAF, LEAF), bf16),
            vmem((NEAR * 2 * LEAF, LEAF), bf16),
            vmem((3, 30, 8, 128), f32),
            vmem((8, 2, 8, 8, 128), f32),
            vmem((6, 2 * RANK, 2 * RANK), bf16),
            vmem((7, FAR * RANK, 2 * RANK), bf16),
            vmem((LEAVES, 2 * RANK, LEAF), bf16),
            vmem((LEAVES, COLS, LEAF), f32),
            dma((8,)), dma((4,)), dma((4,)), dma((2,)), dma((2,)),
            dma((8,)), dma((8,)), dma((8,)), dma((8,)), dma((8,)), dma((8,)),
            pltpu.SemaphoreType.REGULAR,
        ],
        compiler_params=pltpu.CompilerParams(
            collective_id=0, has_side_effects=True, vmem_limit_bytes=48 * 2**20
        ),
    )(
        near_lists.T,
        far_lists.transpose(0, 2, 1),
        coarse_lists.transpose(0, 2, 1),
        vectors,
        points,
        bases.transpose(0, 2, 1),
        transfer,
        coupling,
    )


def solution(mesh):
    in_specs = (
        P("vec", "leaf"),
        P(None, "leaf"),
        P("leaf", None, None),
        P(),
        P(),
        P("leaf", None),
        P(None, "leaf", None),
        P(),
    )
    return jax.shard_map(
        local, mesh=mesh, in_specs=in_specs, out_specs=P("vec", "leaf"), check_vma=False
    )
```

```python
import functools

import jax
import jax.numpy as jnp
from jax import lax
from jax.experimental import pallas as pl
from jax.experimental.pallas import tpu as pltpu
from jax.sharding import PartitionSpec as P

MESH = pl.DeviceIdType.MESH
f32 = jnp.float32
bf16 = jnp.bfloat16
NT = (((1,), (1,)), ((), ()))

N_LEAF = 128
LEAVES = 16
LEAF = 256
RANK = 64
COLS = 16
NEAR = 8
FAR = 4
CUT = 4
SCALE = 5.0 * 1.4426950408889634
WEIGHT = 0.0625
TINY = 1e-30
BASE = (0, 16, 24, 28)
NODES = 30
STRIP = 32


def split(x):
    high = x.astype(bf16)
    return high, (x - high.astype(f32)).astype(bf16)


def stacked(x):
    return jnp.concatenate(split(x), 0)


def fold(d):
    half = d.shape[0] // 2
    return d[:half] + d[half:]


def turned(x):
    return pltpu.roll(x, RANK, 1)


def low_lanes(shape):
    return lax.broadcasted_iota(jnp.int32, shape, 1) < RANK


def pick(a, b):
    return jnp.where(low_lanes(a.shape), a, b)


def both(r):
    return r + turned(r)


def halves(wide):
    high = wide.astype(bf16).astype(f32)
    return jnp.concatenate([high, wide - high], 1).astype(bf16)


def dot(a, b):
    return jnp.dot(a, b, preferred_element_type=f32)


def dot_t(a, b):
    return lax.dot_general(a, b, NT, preferred_element_type=f32)


def kernel(
    near_in, far_in, coarse_in, vec_in, pts_in, bas_in, tra_in, cou_in,
    out_ref,
    near_ref, far_ref, coarse_ref,
    vec, pts, bas, tra, cou, hv, hp, vh, rows, cols, buf_a, buf_b,
    ups, gath, tt, cc, bb, near_out,
    loc, hs, hr, us, ur, zs, zr, ys, yr, cs, cr, chain, here,
):
    me = lax.axis_index("leaf")
    zi, yi, ci = me // 16, lax.rem(me // 2, 8), lax.rem(me, 2)
    left, right = me - 1, me + 1
    sibling = me + 1 - 2 * ci

    def y_peer(k):
        return zi * 16 + lax.rem(yi + k, 8) * 2 + ci

    def signal(sem, peer):
        pl.semaphore_signal(sem, inc=1, device_id={"leaf": peer}, device_id_type=MESH)

    beside = [
        (me > 0, me - 1),
        (me < N_LEAF - 1, me + 1),
        (zi > 0, me - 16),
        (zi < 7, me + 16),
    ]
    barrier = pltpu.get_barrier_semaphore()
    for k in range(1, 8):
        signal(barrier, y_peer(k))
    greeted = 7
    for there, peer in beside:
        greeted += there.astype(jnp.int32)
        pl.when(there)(functools.partial(signal, barrier, peer))

    locals_ = [
        pltpu.make_async_copy(src, dst, loc.at[i])
        for i, (src, dst) in enumerate(
            [
                (tra_in, tra), (cou_in, cou), (vec_in, vec), (bas_in, bas), (pts_in, pts),
                (near_in, near_ref), (far_in, far_ref), (coarse_in, coarse_ref),
            ]
        )
    ]
    for copy in locals_:
        copy.start()

    def remote(src, dst, send, recv, peer):
        return pltpu.make_async_remote_copy(
            src_ref=src, dst_ref=dst, send_sem=send, recv_sem=recv,
            device_id={"leaf": peer}, device_id_type=MESH,
        )

    to_right = [
        remote(vec_in, hv.at[0], hs.at[0], hr.at[0], right),
        remote(pts_in, hp.at[0], hs.at[1], hr.at[1], right),
    ]
    to_left = [
        remote(vec_in, hv.at[1], hs.at[2], hr.at[2], left),
        remote(pts_in, hp.at[1], hs.at[3], hr.at[3], left),
    ]
    mine = ups.at[NODES:2 * NODES]
    up_right = [remote(mine, ups.at[0:NODES], us.at[0], ur.at[0], right)]
    up_left = [remote(mine, ups.at[2 * NODES:3 * NODES], us.at[1], ur.at[1], left)]

    def run(step, copies):
        for copy in copies:
            getattr(copy, step)()

    def send(rightward, leftward, step):
        pl.when(me < N_LEAF - 1)(functools.partial(run, step, rightward))
        pl.when(me > 0)(functools.partial(run, step, leftward))

    def receive(rightward, leftward):
        pl.when(me > 0)(functools.partial(run, "wait_recv", rightward))
        pl.when(me < N_LEAF - 1)(functools.partial(run, "wait_recv", leftward))

    def lower(f, *args):
        for z in range(7):
            pl.when(z < zi)(functools.partial(f, z, *args))

    def higher(f, *args):
        for z in range(1, 8):
            pl.when(z > zi)(functools.partial(f, z, *args))

    def z_block(core, z):
        return gath.at[z, 0] if core == 0 else gath.at[z, 1, yi]

    def y_block(core, y):
        return gath.at[zi, 0, y] if core == 0 else gath.at[:, 1, y]

    def z_send(to, core, step):
        block = z_block(core, zi)
        run(step, [remote(block, block, zs.at[to], zr.at[zi], to * 16 + yi * 2 + core)])

    def z_receive(source, core):
        block = z_block(core, source)
        peer = source * 16 + yi * 2 + core
        run("wait_recv", [remote(block, block, zs.at[source], zr.at[source], peer)])

    def y_send(core, step):
        block = y_block(core, yi)
        for k in range(1, 8):
            run(step, [remote(block, block, ys.at[k], yr.at[k], y_peer(k))])

    def y_receive(core):
        for k in range(1, 8):
            block = y_block(core, lax.rem(yi + 8 - k, 8))
            run("wait_recv", [remote(block, block, ys.at[k], yr.at[k], y_peer(8 - k))])

    def on_core(core, *steps):
        def go():
            for f, *args in steps:
                f(*args)

        pl.when(ci == core)(go)

    half, other = gath.at[:, ci], gath.at[:, 1 - ci]
    c_send = remote(half, half, cs, cr, sibling)
    c_receive = remote(other, other, cs, cr, sibling)

    first = (me == 0) & (lax.axis_index("vec") == 0)

    def enter():
        pl.semaphore_wait(barrier, greeted)
        send(to_right, to_left, "start")

    pl.when(first)(enter)

    locals_[0].wait()
    for k in range(6):
        for c in range(2):
            tt[k, c * RANK:(c + 1) * RANK, :] = halves(tra[k, c])

    locals_[2].wait()
    locals_[3].wait()
    level = []
    for leaf in range(LEAVES):
        s = stacked(vec[:, leaf * LEAF:(leaf + 1) * LEAF])
        vh[LEAVES + leaf] = jnp.concatenate([s, s], 1)
        b = stacked(bas[leaf])
        bb[leaf] = b
        level.append(both(fold(dot_t(s, b))))
    for k in range(CUT + 1):
        for n, u in enumerate(level):
            packed = pick(u[:8], u[8:])
            if k < CUT:
                ups[NODES + BASE[k] + n] = packed
            else:
                gath[zi, ci, yi] = packed
        if k < CUT:
            lhs = jnp.concatenate(
                [pick(level[2 * n], level[2 * n + 1]) for n in range(len(level) // 2)], 0
            )
            u = both(fold(dot(stacked(lhs), tt[k])))
            level = [u[n * COLS:(n + 1) * COLS] for n in range(len(level) // 2)]
    pl.when(jnp.logical_not(first))(enter)
    on_core(0, (y_send, 0, "start"))
    send(up_right, up_left, "start")

    @pl.when(zi > 0)
    def _():
        pl.semaphore_wait(chain, 1)

    pl.when(zi < 7)(functools.partial(signal, chain, me + 16))
    for z in range(7):
        pl.when(z < zi)(functools.partial(signal, here, z * 16 + yi * 2 + ci))
    on_core(1, (lower, z_send, 1, "start"))

    locals_[1].wait()
    for k in range(7):
        for s in range(FAR):
            cc[k, s * RANK:(s + 1) * RANK, :] = halves(cou[k, s])

    def place(m, p):
        x = jnp.broadcast_to(p[0:1, :] * SCALE, (8, LEAF))
        y = jnp.broadcast_to(p[1:2, :] * SCALE, (8, LEAF))
        first = lax.broadcasted_iota(jnp.int32, (8, LEAF), 0) == 0
        cols[m, :, 0:8] = jnp.where(first, x, y).T
        return x, y

    def weights(x, y, m, put):
        x = jnp.concatenate([x] * (STRIP // 8), 0)
        y = jnp.concatenate([y] * (STRIP // 8), 0)
        for r in range(0, LEAF, STRIP):
            sx = jnp.broadcast_to(cols[m, r:r + STRIP, 0:1], (STRIP, LEAF))
            sy = jnp.broadcast_to(cols[m, r:r + STRIP, 1:2], (STRIP, LEAF))
            dx, dy = sx - x, sy - y
            d2 = dx * dx + dy * dy
            if (r // STRIP) % 4 < 3:
                dist = pl.reciprocal(lax.rsqrt(d2), approx=True)
            else:
                d2 = jnp.maximum(d2, TINY)
                dist = d2 * lax.rsqrt(d2)
            put(r, *split(jnp.exp2(-dist)))

    locals_[4].wait()

    def own(i, _):
        for n in range(8):
            t = i * 8 + n
            x, y = place(LEAVES + t, pts[:, pl.ds(pl.multiple_of(t * LEAF, LEAF), LEAF)])
            rows[t, 0] = x
            rows[t, 1] = y
            highs, lows = [], []

            def put(r, high, low):
                highs.append(high)
                lows.append(low)

            weights(x, y, LEAVES + t, put)
            near_out[t] = fold(dot(vh[LEAVES + t], jnp.concatenate(highs + lows, 0)))
        return 0

    lax.fori_loop(0, LEAVES // 8, own, 0)
    for copy in locals_[5:]:
        copy.wait()
    receive(to_right, to_left)

    def others(i, _):
        for n in range(4):
            t = i * 4 + n
            at = pl.ds(pl.multiple_of(t * LEAF, LEAF), LEAF)
            for side in range(2):
                m = 2 * LEAVES * side + t
                place(m, hp[side, :, at])
                s = stacked(hv[side, :, at])
                vh[m] = jnp.concatenate([s, s], 1)
        return 0

    lax.fori_loop(0, LEAVES // 4, others, 0)

    first_leaf = (me - 1) * LEAVES

    def sources(t):
        return [
            jnp.clip(near_ref[j, t] - first_leaf, 0, 3 * LEAVES - 1) for j in range(NEAR)
        ]

    def weigh(t, buf):
        for j, m in enumerate(sources(t)):
            def put(r, high, low, at=j * 2 * LEAF):
                buf[at + r:at + r + STRIP, :] = high
                buf[at + LEAF + r:at + LEAF + r + STRIP, :] = low

            weights(rows[t, 0], rows[t, 1], m, put)

    def apply(t, buf):
        lhs = jnp.concatenate([vh[m] for m in sources(t)], 1)
        near_out[t] = (near_out[t] + fold(dot(lhs, buf[...]))) * WEIGHT

    weigh(0, buf_a)

    def pair(i, _):
        @pl.when(i == 0)
        def _():
            on_core(0, (y_receive, 0), (lower, z_send, 0, "start"))

        @pl.when((i == 2) & (zi < 7))
        def _():
            pl.semaphore_wait(here, 7 - zi)
            on_core(0, (higher, z_send, 0, "start"))
            on_core(1, (higher, z_send, 1, "start"))

        @pl.when(i == 2)
        def _():
            on_core(1, (higher, z_receive, 1), (lower, z_receive, 1), (y_send, 1, "start"))

        @pl.when(i == 6 - 2 * first.astype(jnp.int32))
        def _():
            on_core(0, (higher, z_receive, 0), (lower, z_receive, 0))
            on_core(1, (y_receive, 1))
            c_send.start()

        apply(2 * i, buf_a)
        weigh(2 * i + 1, buf_b)
        apply(2 * i + 1, buf_b)
        weigh(2 * i + 2, buf_a)
        return 0

    lax.fori_loop(0, LEAVES // 2 - 1, pair, 0)

    receive(up_right, up_left)
    c_receive.wait_recv()
    apply(LEAVES - 2, buf_a)
    weigh(LEAVES - 1, buf_b)

    def four(xs):
        rs = [turned(x) for x in xs]
        return jnp.concatenate(
            [
                jnp.concatenate([pick(xs[s], rs[s + 1]), pick(rs[s], xs[s + 1])], 0)
                for s in (0, 2)
            ],
            1,
        )

    def cut_node(n):
        return gath[n >> 4, n & 1, (n >> 1) & 7]

    def couple(lhs, k):
        return both(fold(dot(stacked(lhs), cc[k])))

    far = []
    for k in range(CUT):
        span = LEAVES >> k
        base = (me - 1) * span
        blocks = []
        for n in range(span):
            xs = []
            for s in range(FAR):
                at = jnp.clip(far_ref[k, s, n] - base, 0, 3 * span - 1)
                side = at >> (CUT - k)
                xs.append(ups[at + side * (NODES - span) + BASE[k]])
            blocks.append(four(xs))
        far.append(couple(jnp.concatenate(blocks, 0), k))

    far_4 = couple(four([cut_node(coarse_ref[0, s, me]) for s in range(FAR)]), 4)

    def joined(n):
        a, b = cut_node(2 * n), cut_node(2 * n + 1)
        return jnp.concatenate([pick(a, turned(b)), pick(turned(a), b)], 0)

    mid, top = me // 2, me // 4
    blocks = [joined(coarse_ref[1, s, mid]) for s in range(FAR)]
    for s in range(FAR):
        n = coarse_ref[2, s, top]
        blocks += [joined(2 * n), joined(2 * n + 1)]
    u = both(fold(dot(stacked(jnp.concatenate(blocks, 0)), tt[4])))
    u = [u[n * COLS:(n + 1) * COLS] for n in range(12)]
    far_5 = couple(jnp.concatenate([pick(u[0], u[1]), pick(u[2], u[3])], 1), 5)
    lhs = jnp.concatenate([pick(u[4 + 2 * s], u[5 + 2 * s]) for s in range(FAR)], 0)
    u = both(fold(dot(stacked(lhs), tt[5])))
    u = [u[n * COLS:(n + 1) * COLS] for n in range(4)]
    down = couple(jnp.concatenate([pick(u[0], u[1]), pick(u[2], u[3])], 1), 6)

    def children(d, k):
        r = fold(dot_t(stacked(d), tt[k]))
        t = turned(r)
        return pick(r, t), pick(t, r)

    for k, node, here in ((5, mid, far_5), (4, me, far_4)):
        a, b = children(down, k)
        down = here + jnp.where(lax.rem(node, 2) == 0, a, b)
    for k in range(CUT - 1, -1, -1):
        a, b = children(down, k)
        parts = []
        for n in range(a.shape[0] // COLS):
            at = slice(n * COLS, (n + 1) * COLS)
            parts += [a[at], b[at]]
        down = far[k] + jnp.concatenate(parts, 0)

    apply(LEAVES - 1, buf_b)
    for leaf in range(LEAVES):
        d = stacked(down[leaf * COLS:(leaf + 1) * COLS])
        out_ref[:, leaf * LEAF:(leaf + 1) * LEAF] = near_out[leaf] + fold(dot(d, bb[leaf]))

    send(to_right, to_left, "wait_send")
    send(up_right, up_left, "wait_send")
    for core in range(2):
        on_core(
            core,
            (lower, z_send, core, "wait_send"),
            (higher, z_send, core, "wait_send"),
            (y_send, core, "wait_send"),
        )
    c_send.wait_send()


def local(vectors, points, bases, transfer, coupling, near_lists, far_lists, coarse_lists):
    outside = pl.BlockSpec(memory_space=pltpu.HBM)
    smem = pltpu.SMEM
    vmem = pltpu.VMEM
    dma = pltpu.SemaphoreType.DMA
    return pl.pallas_call(
        kernel,
        out_shape=jax.ShapeDtypeStruct(vectors.shape, f32),
        in_specs=[outside] * 8,
        out_specs=pl.BlockSpec(memory_space=vmem),
        scratch_shapes=[
            smem((NEAR, LEAVES), jnp.int32),
            smem((CUT, FAR, LEAVES), jnp.int32),
            smem((3, FAR, N_LEAF), jnp.int32),
            vmem((COLS, LEAVES * LEAF), f32),
            vmem((2, LEAVES * LEAF), f32),
            vmem((LEAVES, RANK, LEAF), f32),
            vmem((6, 2, RANK, RANK), f32),
            vmem((7, FAR, RANK, RANK), f32),
            vmem((2, COLS, LEAVES * LEAF), f32),
            vmem((2, 2, LEAVES * LEAF), f32),
            vmem((3 * LEAVES, 2 * COLS, 2 * LEAF), bf16),
            vmem((LEAVES, 2, 8, LEAF), f32),
            vmem((3 * LEAVES, LEAF, 128), f32),
            vmem((NEAR * 2 * LEAF, LEAF), bf16),
            vmem((NEAR * 2 * LEAF, LEAF), bf16),
            vmem((3 * NODES, 8, 128), f32),
            vmem((8, 2, 8, 8, 128), f32),
            vmem((6, 2 * RANK, 2 * RANK), bf16),
            vmem((7, FAR * RANK, 2 * RANK), bf16),
            vmem((LEAVES, 2 * RANK, LEAF), bf16),
            vmem((LEAVES, COLS, LEAF), f32),
            dma((8,)), dma((4,)), dma((4,)), dma((2,)), dma((2,)),
            dma((8,)), dma((8,)), dma((8,)), dma((8,)), dma, dma,
            pltpu.SemaphoreType.REGULAR, pltpu.SemaphoreType.REGULAR,
        ],
        compiler_params=pltpu.CompilerParams(
            collective_id=0, has_side_effects=True, vmem_limit_bytes=62 * 2**20
        ),
    )(
        near_lists.T,
        far_lists.transpose(0, 2, 1),
        coarse_lists.transpose(0, 2, 1),
        vectors,
        points,
        bases.transpose(0, 2, 1),
        transfer,
        coupling,
    )


def solution(mesh):
    in_specs = (
        P("vec", "leaf"),
        P(None, "leaf"),
        P("leaf", None, None),
        P(),
        P(),
        P("leaf", None),
        P(None, "leaf", None),
        P(),
    )
    return jax.shard_map(
        local, mesh=mesh, in_specs=in_specs, out_specs=P("vec", "leaf"), check_vma=False
    )
```

```python
import functools

import jax
import jax.numpy as jnp
from jax import lax
from jax.experimental import pallas as pl
from jax.experimental.pallas import tpu as pltpu
from jax.sharding import PartitionSpec as P

MESH = pl.DeviceIdType.MESH
f32 = jnp.float32
bf16 = jnp.bfloat16
NT = (((1,), (1,)), ((), ()))

N_LEAF = 128
LEAVES = 16
LEAF = 256
RANK = 64
COLS = 16
NEAR = 8
FAR = 4
CUT = 4
SCALE = 5.0 * 1.4426950408889634
WEIGHT = 0.0625
TINY = 1e-30
BASE = (0, 16, 24, 28)
NODES = 30
STRIP = 32


def split(x):
    high = x.astype(bf16)
    return high, (x - high.astype(f32)).astype(bf16)


def stacked(x):
    return jnp.concatenate(split(x), 0)


def fold(d):
    half = d.shape[0] // 2
    return d[:half] + d[half:]


def turned(x):
    return pltpu.roll(x, RANK, 1)


def low_lanes(shape):
    return lax.broadcasted_iota(jnp.int32, shape, 1) < RANK


def pick(a, b):
    return jnp.where(low_lanes(a.shape), a, b)


def both(r):
    return r + turned(r)


def halves(wide):
    high = wide.astype(bf16).astype(f32)
    return jnp.concatenate([high, wide - high], 1).astype(bf16)


def dot(a, b):
    return jnp.dot(a, b, preferred_element_type=f32)


def dot_t(a, b):
    return lax.dot_general(a, b, NT, preferred_element_type=f32)


def kernel(
    near_in, far_in, coarse_in, vec_in, pts_in, bas_in, tra_in, cou_in,
    out_ref,
    near_ref, far_ref, coarse_ref,
    vec, pts, bas, tra, cou, hv, hp, vh, rows, cols, buf_a, buf_b,
    ups, gath, tt, cc, bb, near_out,
    loc, hs, hr, us, ur, zs, zr, ys, yr, cs, cr, chain, here,
):
    me = lax.axis_index("leaf")
    zi, yi, ci = me // 16, lax.rem(me // 2, 8), lax.rem(me, 2)
    left, right = me - 1, me + 1
    sibling = me + 1 - 2 * ci

    def y_peer(k):
        return zi * 16 + lax.rem(yi + k, 8) * 2 + ci

    def signal(sem, peer):
        pl.semaphore_signal(sem, inc=1, device_id={"leaf": peer}, device_id_type=MESH)

    beside = [
        (me > 0, me - 1),
        (me < N_LEAF - 1, me + 1),
        (zi > 0, me - 16),
        (zi < 7, me + 16),
    ]
    barrier = pltpu.get_barrier_semaphore()
    for k in range(1, 8):
        signal(barrier, y_peer(k))
    greeted = 7
    for there, peer in beside:
        greeted += there.astype(jnp.int32)
        pl.when(there)(functools.partial(signal, barrier, peer))

    locals_ = [
        pltpu.make_async_copy(src, dst, loc.at[i])
        for i, (src, dst) in enumerate(
            [
                (tra_in, tra), (cou_in, cou), (vec_in, vec), (bas_in, bas), (pts_in, pts),
                (near_in, near_ref), (far_in, far_ref), (coarse_in, coarse_ref),
            ]
        )
    ]
    for copy in locals_:
        copy.start()

    def remote(src, dst, send, recv, peer):
        return pltpu.make_async_remote_copy(
            src_ref=src, dst_ref=dst, send_sem=send, recv_sem=recv,
            device_id={"leaf": peer}, device_id_type=MESH,
        )

    to_right = [
        remote(pts_in, hp.at[0], hs.at[1], hr.at[1], right),
        remote(vec_in, hv.at[0], hs.at[0], hr.at[0], right),
    ]
    to_left = [
        remote(pts_in, hp.at[1], hs.at[3], hr.at[3], left),
        remote(vec_in, hv.at[1], hs.at[2], hr.at[2], left),
    ]
    mine = ups.at[NODES:2 * NODES]
    up_right = [remote(mine, ups.at[0:NODES], us.at[0], ur.at[0], right)]
    up_left = [remote(mine, ups.at[2 * NODES:3 * NODES], us.at[1], ur.at[1], left)]

    def run(step, copies):
        for copy in copies:
            getattr(copy, step)()

    def on_core(core, *steps):
        def go():
            for f, *args in steps:
                f(*args)

        pl.when(ci == core)(go)

    def send(rightward, leftward, step):
        def go_right():
            pl.when(me < N_LEAF - 1)(functools.partial(run, step, rightward))

        def go_left():
            pl.when(me > 0)(functools.partial(run, step, leftward))

        on_core(0, (go_left,), (go_right,))
        on_core(1, (go_right,), (go_left,))

    def receive(rightward, leftward):
        pl.when(me > 0)(functools.partial(run, "wait_recv", rightward))
        pl.when(me < N_LEAF - 1)(functools.partial(run, "wait_recv", leftward))

    def lower(f, *args):
        for z in range(7):
            pl.when(z < zi)(functools.partial(f, z, *args))

    def higher(f, *args):
        for z in range(1, 8):
            pl.when(z > zi)(functools.partial(f, z, *args))

    def z_block(core, z):
        return gath.at[z, 0] if core == 0 else gath.at[z, 1, yi]

    def y_block(core, y):
        return gath.at[zi, 0, y] if core == 0 else gath.at[:, 1, y]

    def z_send(to, core, step):
        block = z_block(core, zi)
        run(step, [remote(block, block, zs.at[to], zr.at[zi], to * 16 + yi * 2 + core)])

    def z_receive(source, core):
        block = z_block(core, source)
        peer = source * 16 + yi * 2 + core
        run("wait_recv", [remote(block, block, zs.at[source], zr.at[source], peer)])

    def y_send(core, step):
        block = y_block(core, yi)
        for k in range(1, 8):
            run(step, [remote(block, block, ys.at[k], yr.at[k], y_peer(k))])

    def y_receive(core):
        for k in range(1, 8):
            block = y_block(core, lax.rem(yi + 8 - k, 8))
            run("wait_recv", [remote(block, block, ys.at[k], yr.at[k], y_peer(8 - k))])

    half, other = gath.at[:, ci], gath.at[:, 1 - ci]
    c_send = remote(half, half, cs, cr, sibling)
    c_receive = remote(other, other, cs, cr, sibling)

    first = (me == 0) & (lax.axis_index("vec") == 0)

    def enter():
        pl.semaphore_wait(barrier, greeted)
        send(to_right, to_left, "start")

    pl.when(first)(enter)

    locals_[0].wait()
    for k in range(6):
        for c in range(2):
            tt[k, c * RANK:(c + 1) * RANK, :] = halves(tra[k, c])

    locals_[2].wait()
    locals_[3].wait()
    level = []
    for leaf in range(LEAVES):
        s = stacked(vec[:, leaf * LEAF:(leaf + 1) * LEAF])
        vh[LEAVES + leaf] = jnp.concatenate([s, s], 1)
        b = stacked(bas[leaf])
        bb[leaf] = b
        level.append(both(fold(dot_t(s, b))))
    for k in range(CUT + 1):
        for n, u in enumerate(level):
            packed = pick(u[:8], u[8:])
            if k < CUT:
                ups[NODES + BASE[k] + n] = packed
            else:
                gath[zi, ci, yi] = packed
        if k < CUT:
            lhs = jnp.concatenate(
                [pick(level[2 * n], level[2 * n + 1]) for n in range(len(level) // 2)], 0
            )
            u = both(fold(dot(stacked(lhs), tt[k])))
            level = [u[n * COLS:(n + 1) * COLS] for n in range(len(level) // 2)]
    pl.when(jnp.logical_not(first))(enter)
    on_core(0, (y_send, 0, "start"))
    send(up_right, up_left, "start")

    @pl.when(zi > 0)
    def _():
        pl.semaphore_wait(chain, 1)

    pl.when(zi < 7)(functools.partial(signal, chain, me + 16))
    for z in range(7):
        pl.when(z < zi)(functools.partial(signal, here, z * 16 + yi * 2 + ci))
    on_core(1, (lower, z_send, 1, "start"))

    locals_[1].wait()
    for k in range(7):
        for s in range(FAR):
            cc[k, s * RANK:(s + 1) * RANK, :] = halves(cou[k, s])

    def place(m, p):
        x = jnp.broadcast_to(p[0:1, :] * SCALE, (8, LEAF))
        y = jnp.broadcast_to(p[1:2, :] * SCALE, (8, LEAF))
        first = lax.broadcasted_iota(jnp.int32, (8, LEAF), 0) == 0
        cols[m, :, 0:8] = jnp.where(first, x, y).T
        return x, y

    def weights(x, y, m, put):
        x = jnp.concatenate([x] * (STRIP // 8), 0)
        y = jnp.concatenate([y] * (STRIP // 8), 0)
        for r in range(0, LEAF, STRIP):
            sx = jnp.broadcast_to(cols[m, r:r + STRIP, 0:1], (STRIP, LEAF))
            sy = jnp.broadcast_to(cols[m, r:r + STRIP, 1:2], (STRIP, LEAF))
            dx, dy = sx - x, sy - y
            d2 = dx * dx + dy * dy
            if (r // STRIP) % 4 < 3:
                dist = pl.reciprocal(lax.rsqrt(d2), approx=True)
            else:
                d2 = jnp.maximum(d2, TINY)
                dist = d2 * lax.rsqrt(d2)
            put(r, *split(jnp.exp2(-dist)))

    locals_[4].wait()

    def own(i, _):
        for n in range(8):
            t = i * 8 + n
            x, y = place(LEAVES + t, pts[:, pl.ds(pl.multiple_of(t * LEAF, LEAF), LEAF)])
            rows[t, 0] = x
            rows[t, 1] = y
            highs, lows = [], []

            def put(r, high, low):
                highs.append(high)
                lows.append(low)

            weights(x, y, LEAVES + t, put)
            near_out[t] = fold(dot(vh[LEAVES + t], jnp.concatenate(highs + lows, 0)))
        return 0

    lax.fori_loop(0, LEAVES // 8, own, 0)
    for copy in locals_[5:]:
        copy.wait()
    receive(to_right[:1], to_left[:1])

    def others(i, _):
        for n in range(4):
            t = i * 4 + n
            at = pl.ds(pl.multiple_of(t * LEAF, LEAF), LEAF)
            for side in range(2):
                m = 2 * LEAVES * side + t
                place(m, hp[side, :, at])
        return 0

    lax.fori_loop(0, LEAVES // 4, others, 0)

    first_leaf = (me - 1) * LEAVES

    def sources(t):
        return [
            jnp.clip(near_ref[j, t] - first_leaf, 0, 3 * LEAVES - 1) for j in range(NEAR)
        ]

    def weigh(t, buf):
        for j, m in enumerate(sources(t)):
            def put(r, high, low, at=j * 2 * LEAF):
                buf[at + r:at + r + STRIP, :] = high
                buf[at + LEAF + r:at + LEAF + r + STRIP, :] = low

            weights(rows[t, 0], rows[t, 1], m, put)

    def apply(t, buf):
        lhs = jnp.concatenate([vh[m] for m in sources(t)], 1)
        near_out[t] = (near_out[t] + fold(dot(lhs, buf[...]))) * WEIGHT

    weigh(0, buf_a)
    receive(to_right[1:], to_left[1:])

    def parts(i, _):
        for n in range(8):
            t = i * 8 + n
            at = pl.ds(pl.multiple_of(t * LEAF, LEAF), LEAF)
            for side in range(2):
                s = stacked(hv[side, :, at])
                vh[2 * LEAVES * side + t] = jnp.concatenate([s, s], 1)
        return 0

    lax.fori_loop(0, LEAVES // 8, parts, 0)

    def pair(i, _):
        @pl.when(i == 0)
        def _():
            on_core(0, (y_receive, 0), (lower, z_send, 0, "start"))

        @pl.when((i == 2) & (zi < 7))
        def _():
            pl.semaphore_wait(here, 7 - zi)
            on_core(0, (higher, z_send, 0, "start"))
            on_core(1, (higher, z_send, 1, "start"))

        @pl.when(i == 3)
        def _():
            on_core(1, (higher, z_receive, 1), (lower, z_receive, 1), (y_send, 1, "start"))

        @pl.when(i == 6 - 2 * first.astype(jnp.int32))
        def _():
            on_core(0, (higher, z_receive, 0), (lower, z_receive, 0))
            on_core(1, (y_receive, 1))
            c_send.start()

        apply(2 * i, buf_a)
        weigh(2 * i + 1, buf_b)
        apply(2 * i + 1, buf_b)
        weigh(2 * i + 2, buf_a)
        return 0

    lax.fori_loop(0, LEAVES // 2 - 1, pair, 0)

    receive(up_right, up_left)
    c_receive.wait_recv()
    apply(LEAVES - 2, buf_a)
    weigh(LEAVES - 1, buf_b)

    def four(xs):
        rs = [turned(x) for x in xs]
        return jnp.concatenate(
            [
                jnp.concatenate([pick(xs[s], rs[s + 1]), pick(rs[s], xs[s + 1])], 0)
                for s in (0, 2)
            ],
            1,
        )

    def cut_node(n):
        return gath[n >> 4, n & 1, (n >> 1) & 7]

    def couple(lhs, k):
        return both(fold(dot(stacked(lhs), cc[k])))

    far = []
    for k in range(CUT):
        span = LEAVES >> k
        base = (me - 1) * span
        blocks = []
        for n in range(span):
            xs = []
            for s in range(FAR):
                at = jnp.clip(far_ref[k, s, n] - base, 0, 3 * span - 1)
                side = at >> (CUT - k)
                xs.append(ups[at + side * (NODES - span) + BASE[k]])
            blocks.append(four(xs))
        far.append(couple(jnp.concatenate(blocks, 0), k))

    far_4 = couple(four([cut_node(coarse_ref[0, s, me]) for s in range(FAR)]), 4)

    def joined(n):
        a, b = cut_node(2 * n), cut_node(2 * n + 1)
        return jnp.concatenate([pick(a, turned(b)), pick(turned(a), b)], 0)

    mid, top = me // 2, me // 4
    blocks = [joined(coarse_ref[1, s, mid]) for s in range(FAR)]
    for s in range(FAR):
        n = coarse_ref[2, s, top]
        blocks += [joined(2 * n), joined(2 * n + 1)]
    u = both(fold(dot(stacked(jnp.concatenate(blocks, 0)), tt[4])))
    u = [u[n * COLS:(n + 1) * COLS] for n in range(12)]
    far_5 = couple(jnp.concatenate([pick(u[0], u[1]), pick(u[2], u[3])], 1), 5)
    lhs = jnp.concatenate([pick(u[4 + 2 * s], u[5 + 2 * s]) for s in range(FAR)], 0)
    u = both(fold(dot(stacked(lhs), tt[5])))
    u = [u[n * COLS:(n + 1) * COLS] for n in range(4)]
    down = couple(jnp.concatenate([pick(u[0], u[1]), pick(u[2], u[3])], 1), 6)

    def children(d, k):
        r = fold(dot_t(stacked(d), tt[k]))
        t = turned(r)
        return pick(r, t), pick(t, r)

    for k, node, here in ((5, mid, far_5), (4, me, far_4)):
        a, b = children(down, k)
        down = here + jnp.where(lax.rem(node, 2) == 0, a, b)
    for k in range(CUT - 1, -1, -1):
        a, b = children(down, k)
        parts = []
        for n in range(a.shape[0] // COLS):
            at = slice(n * COLS, (n + 1) * COLS)
            parts += [a[at], b[at]]
        down = far[k] + jnp.concatenate(parts, 0)

    apply(LEAVES - 1, buf_b)
    for leaf in range(LEAVES):
        d = stacked(down[leaf * COLS:(leaf + 1) * COLS])
        out_ref[:, leaf * LEAF:(leaf + 1) * LEAF] = near_out[leaf] + fold(dot(d, bb[leaf]))

    send(to_right, to_left, "wait_send")
    send(up_right, up_left, "wait_send")
    for core in range(2):
        on_core(
            core,
            (lower, z_send, core, "wait_send"),
            (higher, z_send, core, "wait_send"),
            (y_send, core, "wait_send"),
        )
    c_send.wait_send()


def local(vectors, points, bases, transfer, coupling, near_lists, far_lists, coarse_lists):
    outside = pl.BlockSpec(memory_space=pltpu.HBM)
    smem = pltpu.SMEM
    vmem = pltpu.VMEM
    dma = pltpu.SemaphoreType.DMA
    return pl.pallas_call(
        kernel,
        out_shape=jax.ShapeDtypeStruct(vectors.shape, f32),
        in_specs=[outside] * 8,
        out_specs=pl.BlockSpec(memory_space=vmem),
        scratch_shapes=[
            smem((NEAR, LEAVES), jnp.int32),
            smem((CUT, FAR, LEAVES), jnp.int32),
            smem((3, FAR, N_LEAF), jnp.int32),
            vmem((COLS, LEAVES * LEAF), f32),
            vmem((2, LEAVES * LEAF), f32),
            vmem((LEAVES, RANK, LEAF), f32),
            vmem((6, 2, RANK, RANK), f32),
            vmem((7, FAR, RANK, RANK), f32),
            vmem((2, COLS, LEAVES * LEAF), f32),
            vmem((2, 2, LEAVES * LEAF), f32),
            vmem((3 * LEAVES, 2 * COLS, 2 * LEAF), bf16),
            vmem((LEAVES, 2, 8, LEAF), f32),
            vmem((3 * LEAVES, LEAF, 128), f32),
            vmem((NEAR * 2 * LEAF, LEAF), bf16),
            vmem((NEAR * 2 * LEAF, LEAF), bf16),
            vmem((3 * NODES, 8, 128), f32),
            vmem((8, 2, 8, 8, 128), f32),
            vmem((6, 2 * RANK, 2 * RANK), bf16),
            vmem((7, FAR * RANK, 2 * RANK), bf16),
            vmem((LEAVES, 2 * RANK, LEAF), bf16),
            vmem((LEAVES, COLS, LEAF), f32),
            dma((8,)), dma((4,)), dma((4,)), dma((2,)), dma((2,)),
            dma((8,)), dma((8,)), dma((8,)), dma((8,)), dma, dma,
            pltpu.SemaphoreType.REGULAR, pltpu.SemaphoreType.REGULAR,
        ],
        compiler_params=pltpu.CompilerParams(
            collective_id=0, has_side_effects=True, vmem_limit_bytes=62 * 2**20
        ),
    )(
        near_lists.T,
        far_lists.transpose(0, 2, 1),
        coarse_lists.transpose(0, 2, 1),
        vectors,
        points,
        bases.transpose(0, 2, 1),
        transfer,
        coupling,
    )


def solution(mesh):
    in_specs = (
        P("vec", "leaf"),
        P(None, "leaf"),
        P("leaf", None, None),
        P(),
        P(),
        P("leaf", None),
        P(None, "leaf", None),
        P(),
    )
    return jax.shard_map(
        local, mesh=mesh, in_specs=in_specs, out_specs=P("vec", "leaf"), check_vma=False
    )
```

```python
import functools

import jax
import jax.numpy as jnp
from jax import lax
from jax.experimental import pallas as pl
from jax.experimental.pallas import tpu as pltpu
from jax.sharding import PartitionSpec as P

MESH = pl.DeviceIdType.MESH
f32 = jnp.float32
bf16 = jnp.bfloat16
NT = (((1,), (1,)), ((), ()))

N_LEAF = 128
LEAVES = 16
LEAF = 256
RANK = 64
COLS = 16
NEAR = 8
FAR = 4
CUT = 4
SCALE = 5.0 * 1.4426950408889634
WEIGHT = 0.0625
TINY = 1e-30
BASE = (0, 16, 24, 28)
NODES = 30
STRIP = 32


def split(x):
    high = x.astype(bf16)
    return high, (x - high.astype(f32)).astype(bf16)


def stacked(x):
    return jnp.concatenate(split(x), 0)


def fold(d):
    half = d.shape[0] // 2
    return d[:half] + d[half:]


def turned(x):
    return pltpu.roll(x, RANK, 1)


def low_lanes(shape):
    return lax.broadcasted_iota(jnp.int32, shape, 1) < RANK


def pick(a, b):
    return jnp.where(low_lanes(a.shape), a, b)


def both(r):
    return r + turned(r)


def halves(wide):
    high = wide.astype(bf16).astype(f32)
    return jnp.concatenate([high, wide - high], 1).astype(bf16)


def dot(a, b):
    return jnp.dot(a, b, preferred_element_type=f32)


def dot_t(a, b):
    return lax.dot_general(a, b, NT, preferred_element_type=f32)


def kernel(
    near_in, far_in, coarse_in, vec_in, pts_in, bas_in, tra_in, cou_in,
    out_ref,
    near_ref, far_ref, coarse_ref,
    vec, pts, bas, tra, cou, hv, hp, vh, rows, cols, buf_a, buf_b,
    ups, gath, tt, cc, bb, near_out,
    loc, hs, hr, us, ur, zs, zr, ys, yr, cs, cr, chain, here, late,
):
    me = lax.axis_index("leaf")
    zi, yi, ci = me // 16, lax.rem(me // 2, 8), lax.rem(me, 2)
    left, right = me - 1, me + 1
    sibling = me + 1 - 2 * ci

    def y_peer(k):
        return zi * 16 + lax.rem(yi + k, 8) * 2 + ci

    def signal(sem, peer):
        pl.semaphore_signal(sem, inc=1, device_id={"leaf": peer}, device_id_type=MESH)

    beside = [
        (me > 0, me - 1),
        (me < N_LEAF - 1, me + 1),
        (zi > 0, me - 16),
        (zi < 7, me + 16),
    ]
    vi = lax.axis_index("vec")
    first = (me == 0) & (vi == 0)
    after_first = (zi == 0) & (ci == 0) & (yi > 0) & (vi == 0)

    barrier = pltpu.get_barrier_semaphore()

    def greet_y(sem):
        for k in range(1, 8):
            signal(sem, y_peer(k))

    pl.when(jnp.logical_not(first))(functools.partial(greet_y, barrier))
    greeted = 7 - after_first.astype(jnp.int32)
    for there, peer in beside:
        greeted += there.astype(jnp.int32)
        pl.when(there)(functools.partial(signal, barrier, peer))

    locals_ = [
        pltpu.make_async_copy(src, dst, loc.at[i])
        for i, (src, dst) in enumerate(
            [
                (tra_in, tra), (cou_in, cou), (vec_in, vec), (bas_in, bas), (pts_in, pts),
                (near_in, near_ref), (far_in, far_ref), (coarse_in, coarse_ref),
            ]
        )
    ]
    for copy in locals_:
        copy.start()

    def remote(src, dst, send, recv, peer):
        return pltpu.make_async_remote_copy(
            src_ref=src, dst_ref=dst, send_sem=send, recv_sem=recv,
            device_id={"leaf": peer}, device_id_type=MESH,
        )

    to_right = [
        remote(pts_in, hp.at[0], hs.at[1], hr.at[1], right),
        remote(vec_in, hv.at[0], hs.at[0], hr.at[0], right),
    ]
    to_left = [
        remote(pts_in, hp.at[1], hs.at[3], hr.at[3], left),
        remote(vec_in, hv.at[1], hs.at[2], hr.at[2], left),
    ]
    mine = ups.at[NODES:2 * NODES]
    up_right = [remote(mine, ups.at[0:NODES], us.at[0], ur.at[0], right)]
    up_left = [remote(mine, ups.at[2 * NODES:3 * NODES], us.at[1], ur.at[1], left)]

    def run(step, copies):
        for copy in copies:
            getattr(copy, step)()

    def on_core(core, *steps):
        def go():
            for f, *args in steps:
                f(*args)

        pl.when(ci == core)(go)

    def send(rightward, leftward, step):
        def go_right():
            pl.when(me < N_LEAF - 1)(functools.partial(run, step, rightward))

        def go_left():
            pl.when(me > 0)(functools.partial(run, step, leftward))

        on_core(0, (go_left,), (go_right,))
        on_core(1, (go_right,), (go_left,))

    def receive(rightward, leftward):
        pl.when(me > 0)(functools.partial(run, "wait_recv", rightward))
        pl.when(me < N_LEAF - 1)(functools.partial(run, "wait_recv", leftward))

    def lower(f, *args):
        for z in range(7):
            pl.when(z < zi)(functools.partial(f, z, *args))

    def higher(f, *args):
        for z in range(1, 8):
            pl.when(z > zi)(functools.partial(f, z, *args))

    def z_block(core, z):
        return gath.at[z, 0] if core == 0 else gath.at[z, 1, yi]

    def y_block(core, y):
        return gath.at[zi, 0, y] if core == 0 else gath.at[:, 1, y]

    def z_send(to, core, step):
        block = z_block(core, zi)
        run(step, [remote(block, block, zs.at[to], zr.at[zi], to * 16 + yi * 2 + core)])

    def z_receive(source, core):
        block = z_block(core, source)
        peer = source * 16 + yi * 2 + core
        run("wait_recv", [remote(block, block, zs.at[source], zr.at[source], peer)])

    def y_send(core, step):
        block = y_block(core, yi)
        for k in range(1, 8):
            run(step, [remote(block, block, ys.at[k], yr.at[k], y_peer(k))])

    def y_to(k):
        block = y_block(0, yi)
        remote(block, block, ys.at[k], yr.at[k], y_peer(k)).start()

    def y_early():
        for k in range(1, 8):
            put_off = after_first & (lax.rem(yi + k, 8) == 0)
            pl.when(jnp.logical_not(put_off))(functools.partial(y_to, k))

    def y_late():
        @pl.when(after_first)
        def _():
            pl.semaphore_wait(late, 1)
            y_to(8 - yi)

    def y_receive(core):
        for k in range(1, 8):
            block = y_block(core, lax.rem(yi + 8 - k, 8))
            run("wait_recv", [remote(block, block, ys.at[k], yr.at[k], y_peer(8 - k))])

    half, other = gath.at[:, ci], gath.at[:, 1 - ci]
    c_send = remote(half, half, cs, cr, sibling)
    c_receive = remote(other, other, cs, cr, sibling)

    def enter():
        pl.semaphore_wait(barrier, greeted)
        send(to_right, to_left, "start")
        pl.when(first)(functools.partial(greet_y, late))

    pl.when(first)(enter)

    locals_[0].wait()
    for k in range(6):
        for c in range(2):
            tt[k, c * RANK:(c + 1) * RANK, :] = halves(tra[k, c])

    locals_[2].wait()
    locals_[3].wait()
    level = []
    for leaf in range(LEAVES):
        s = stacked(vec[:, leaf * LEAF:(leaf + 1) * LEAF])
        vh[LEAVES + leaf] = jnp.concatenate([s, s], 1)
        b = stacked(bas[leaf])
        bb[leaf] = b
        level.append(both(fold(dot_t(s, b))))
    for k in range(CUT + 1):
        for n, u in enumerate(level):
            packed = pick(u[:8], u[8:])
            if k < CUT:
                ups[NODES + BASE[k] + n] = packed
            else:
                gath[zi, ci, yi] = packed
        if k < CUT:
            lhs = jnp.concatenate(
                [pick(level[2 * n], level[2 * n + 1]) for n in range(len(level) // 2)], 0
            )
            u = both(fold(dot(stacked(lhs), tt[k])))
            level = [u[n * COLS:(n + 1) * COLS] for n in range(len(level) // 2)]
    patient = (yi == 0) & jnp.logical_not(first)

    def greet():
        pl.when(jnp.logical_not(first))(enter)
        on_core(0, (y_early,))
        send(up_right, up_left, "start")

        @pl.when(zi > 0)
        def _():
            pl.semaphore_wait(chain, 1)

        pl.when(zi < 7)(functools.partial(signal, chain, me + 16))
        for z in range(7):
            pl.when(z < zi)(functools.partial(signal, here, z * 16 + yi * 2 + ci))
        on_core(1, (lower, z_send, 1, "start"))

    pl.when(jnp.logical_not(patient))(greet)

    locals_[1].wait()
    for k in range(7):
        for s in range(FAR):
            cc[k, s * RANK:(s + 1) * RANK, :] = halves(cou[k, s])

    def place(m, p):
        x = jnp.broadcast_to(p[0:1, :] * SCALE, (8, LEAF))
        y = jnp.broadcast_to(p[1:2, :] * SCALE, (8, LEAF))
        first = lax.broadcasted_iota(jnp.int32, (8, LEAF), 0) == 0
        cols[m, :, 0:8] = jnp.where(first, x, y).T
        return x, y

    def weights(x, y, m, put):
        x = jnp.concatenate([x] * (STRIP // 8), 0)
        y = jnp.concatenate([y] * (STRIP // 8), 0)
        for r in range(0, LEAF, STRIP):
            sx = jnp.broadcast_to(cols[m, r:r + STRIP, 0:1], (STRIP, LEAF))
            sy = jnp.broadcast_to(cols[m, r:r + STRIP, 1:2], (STRIP, LEAF))
            dx, dy = sx - x, sy - y
            d2 = dx * dx + dy * dy
            if (r // STRIP) % 4 < 3:
                dist = pl.reciprocal(lax.rsqrt(d2), approx=True)
            else:
                d2 = jnp.maximum(d2, TINY)
                dist = d2 * lax.rsqrt(d2)
            put(r, *split(jnp.exp2(-dist)))

    locals_[4].wait()

    def own(i, _):
        for n in range(8):
            t = i * 8 + n
            x, y = place(LEAVES + t, pts[:, pl.ds(pl.multiple_of(t * LEAF, LEAF), LEAF)])
            rows[t, 0] = x
            rows[t, 1] = y
            highs, lows = [], []

            def put(r, high, low):
                highs.append(high)
                lows.append(low)

            weights(x, y, LEAVES + t, put)
            near_out[t] = fold(dot(vh[LEAVES + t], jnp.concatenate(highs + lows, 0)))
        return 0

    def own_part(i, _):
        pl.when((i == 1) & patient)(greet)
        return own(i, _)

    lax.fori_loop(0, LEAVES // 8, own_part, 0)
    for copy in locals_[5:]:
        copy.wait()
    receive(to_right[:1], to_left[:1])

    def others(i, _):
        for n in range(4):
            t = i * 4 + n
            at = pl.ds(pl.multiple_of(t * LEAF, LEAF), LEAF)
            for side in range(2):
                m = 2 * LEAVES * side + t
                place(m, hp[side, :, at])
        return 0

    lax.fori_loop(0, LEAVES // 4, others, 0)

    first_leaf = (me - 1) * LEAVES

    def sources(t):
        return [
            jnp.clip(near_ref[j, t] - first_leaf, 0, 3 * LEAVES - 1) for j in range(NEAR)
        ]

    def weigh(t, buf):
        for j, m in enumerate(sources(t)):
            def put(r, high, low, at=j * 2 * LEAF):
                buf[at + r:at + r + STRIP, :] = high
                buf[at + LEAF + r:at + LEAF + r + STRIP, :] = low

            weights(rows[t, 0], rows[t, 1], m, put)

    def apply(t, buf):
        lhs = jnp.concatenate([vh[m] for m in sources(t)], 1)
        near_out[t] = (near_out[t] + fold(dot(lhs, buf[...]))) * WEIGHT

    weigh(0, buf_a)
    receive(to_right[1:], to_left[1:])

    def parts(i, _):
        for n in range(8):
            t = i * 8 + n
            at = pl.ds(pl.multiple_of(t * LEAF, LEAF), LEAF)
            for side in range(2):
                s = stacked(hv[side, :, at])
                vh[2 * LEAVES * side + t] = jnp.concatenate([s, s], 1)
        return 0

    lax.fori_loop(0, LEAVES // 8, parts, 0)

    def pair(i, _):
        @pl.when(i == 0)
        def _():
            on_core(0, (y_late,), (y_receive, 0), (lower, z_send, 0, "start"))

        @pl.when((i == 2) & (zi < 7))
        def _():
            pl.semaphore_wait(here, 7 - zi)
            on_core(0, (higher, z_send, 0, "start"))
            on_core(1, (higher, z_send, 1, "start"))

        @pl.when(i == 3)
        def _():
            on_core(1, (higher, z_receive, 1), (lower, z_receive, 1), (y_send, 1, "start"))

        @pl.when(i == 6 - 2 * first.astype(jnp.int32))
        def _():
            on_core(0, (higher, z_receive, 0), (lower, z_receive, 0))
            on_core(1, (y_receive, 1))
            c_send.start()

        apply(2 * i, buf_a)
        weigh(2 * i + 1, buf_b)
        apply(2 * i + 1, buf_b)
        weigh(2 * i + 2, buf_a)
        return 0

    lax.fori_loop(0, LEAVES // 2 - 1, pair, 0)

    receive(up_right, up_left)
    c_receive.wait_recv()
    apply(LEAVES - 2, buf_a)
    weigh(LEAVES - 1, buf_b)

    def four(xs):
        rs = [turned(x) for x in xs]
        return jnp.concatenate(
            [
                jnp.concatenate([pick(xs[s], rs[s + 1]), pick(rs[s], xs[s + 1])], 0)
                for s in (0, 2)
            ],
            1,
        )

    def cut_node(n):
        return gath[n >> 4, n & 1, (n >> 1) & 7]

    def couple(lhs, k):
        return both(fold(dot(stacked(lhs), cc[k])))

    far = []
    for k in range(CUT):
        span = LEAVES >> k
        base = (me - 1) * span
        blocks = []
        for n in range(span):
            xs = []
            for s in range(FAR):
                at = jnp.clip(far_ref[k, s, n] - base, 0, 3 * span - 1)
                side = at >> (CUT - k)
                xs.append(ups[at + side * (NODES - span) + BASE[k]])
            blocks.append(four(xs))
        far.append(couple(jnp.concatenate(blocks, 0), k))

    far_4 = couple(four([cut_node(coarse_ref[0, s, me]) for s in range(FAR)]), 4)

    def joined(n):
        a, b = cut_node(2 * n), cut_node(2 * n + 1)
        return jnp.concatenate([pick(a, turned(b)), pick(turned(a), b)], 0)

    mid, top = me // 2, me // 4
    blocks = [joined(coarse_ref[1, s, mid]) for s in range(FAR)]
    for s in range(FAR):
        n = coarse_ref[2, s, top]
        blocks += [joined(2 * n), joined(2 * n + 1)]
    u = both(fold(dot(stacked(jnp.concatenate(blocks, 0)), tt[4])))
    u = [u[n * COLS:(n + 1) * COLS] for n in range(12)]
    far_5 = couple(jnp.concatenate([pick(u[0], u[1]), pick(u[2], u[3])], 1), 5)
    lhs = jnp.concatenate([pick(u[4 + 2 * s], u[5 + 2 * s]) for s in range(FAR)], 0)
    u = both(fold(dot(stacked(lhs), tt[5])))
    u = [u[n * COLS:(n + 1) * COLS] for n in range(4)]
    down = couple(jnp.concatenate([pick(u[0], u[1]), pick(u[2], u[3])], 1), 6)

    def children(d, k):
        r = fold(dot_t(stacked(d), tt[k]))
        t = turned(r)
        return pick(r, t), pick(t, r)

    for k, node, here in ((5, mid, far_5), (4, me, far_4)):
        a, b = children(down, k)
        down = here + jnp.where(lax.rem(node, 2) == 0, a, b)
    for k in range(CUT - 1, -1, -1):
        a, b = children(down, k)
        parts = []
        for n in range(a.shape[0] // COLS):
            at = slice(n * COLS, (n + 1) * COLS)
            parts += [a[at], b[at]]
        down = far[k] + jnp.concatenate(parts, 0)

    apply(LEAVES - 1, buf_b)
    for leaf in range(LEAVES):
        d = stacked(down[leaf * COLS:(leaf + 1) * COLS])
        out_ref[:, leaf * LEAF:(leaf + 1) * LEAF] = near_out[leaf] + fold(dot(d, bb[leaf]))

    send(to_right, to_left, "wait_send")
    send(up_right, up_left, "wait_send")
    for core in range(2):
        on_core(
            core,
            (lower, z_send, core, "wait_send"),
            (higher, z_send, core, "wait_send"),
            (y_send, core, "wait_send"),
        )
    c_send.wait_send()


def local(vectors, points, bases, transfer, coupling, near_lists, far_lists, coarse_lists):
    outside = pl.BlockSpec(memory_space=pltpu.HBM)
    smem = pltpu.SMEM
    vmem = pltpu.VMEM
    dma = pltpu.SemaphoreType.DMA
    return pl.pallas_call(
        kernel,
        out_shape=jax.ShapeDtypeStruct(vectors.shape, f32),
        in_specs=[outside] * 8,
        out_specs=pl.BlockSpec(memory_space=vmem),
        scratch_shapes=[
            smem((NEAR, LEAVES), jnp.int32),
            smem((CUT, FAR, LEAVES), jnp.int32),
            smem((3, FAR, N_LEAF), jnp.int32),
            vmem((COLS, LEAVES * LEAF), f32),
            vmem((2, LEAVES * LEAF), f32),
            vmem((LEAVES, RANK, LEAF), f32),
            vmem((6, 2, RANK, RANK), f32),
            vmem((7, FAR, RANK, RANK), f32),
            vmem((2, COLS, LEAVES * LEAF), f32),
            vmem((2, 2, LEAVES * LEAF), f32),
            vmem((3 * LEAVES, 2 * COLS, 2 * LEAF), bf16),
            vmem((LEAVES, 2, 8, LEAF), f32),
            vmem((3 * LEAVES, LEAF, 128), f32),
            vmem((NEAR * 2 * LEAF, LEAF), bf16),
            vmem((NEAR * 2 * LEAF, LEAF), bf16),
            vmem((3 * NODES, 8, 128), f32),
            vmem((8, 2, 8, 8, 128), f32),
            vmem((6, 2 * RANK, 2 * RANK), bf16),
            vmem((7, FAR * RANK, 2 * RANK), bf16),
            vmem((LEAVES, 2 * RANK, LEAF), bf16),
            vmem((LEAVES, COLS, LEAF), f32),
            dma((8,)), dma((4,)), dma((4,)), dma((2,)), dma((2,)),
            dma((8,)), dma((8,)), dma((8,)), dma((8,)), dma, dma,
            pltpu.SemaphoreType.REGULAR, pltpu.SemaphoreType.REGULAR,
            pltpu.SemaphoreType.REGULAR,
        ],
        compiler_params=pltpu.CompilerParams(
            collective_id=0, has_side_effects=True, vmem_limit_bytes=62 * 2**20
        ),
    )(
        near_lists.T,
        far_lists.transpose(0, 2, 1),
        coarse_lists.transpose(0, 2, 1),
        vectors,
        points,
        bases.transpose(0, 2, 1),
        transfer,
        coupling,
    )


def solution(mesh):
    in_specs = (
        P("vec", "leaf"),
        P(None, "leaf"),
        P("leaf", None, None),
        P(),
        P(),
        P("leaf", None),
        P(None, "leaf", None),
        P(),
    )
    return jax.shard_map(
        local, mesh=mesh, in_specs=in_specs, out_specs=P("vec", "leaf"), check_vma=False
    )
```

```python
import functools

import jax
import jax.numpy as jnp
from jax import lax
from jax.experimental import pallas as pl
from jax.experimental.pallas import tpu as pltpu
from jax.sharding import PartitionSpec as P

MESH = pl.DeviceIdType.MESH
f32 = jnp.float32
bf16 = jnp.bfloat16
NT = (((1,), (1,)), ((), ()))

N_LEAF = 128
LEAVES = 16
LEAF = 256
RANK = 64
COLS = 16
NEAR = 8
FAR = 4
CUT = 4
SCALE = 5.0 * 1.4426950408889634
WEIGHT = 0.0625
TINY = 1e-30
BASE = (0, 16, 24, 28)
NODES = 30
STRIP = 32


def split(x):
    high = x.astype(bf16)
    return high, (x - high.astype(f32)).astype(bf16)


def stacked(x):
    return jnp.concatenate(split(x), 0)


def fold(d):
    half = d.shape[0] // 2
    return d[:half] + d[half:]


def turned(x):
    return pltpu.roll(x, RANK, 1)


def low_lanes(shape):
    return lax.broadcasted_iota(jnp.int32, shape, 1) < RANK


def pick(a, b):
    return jnp.where(low_lanes(a.shape), a, b)


def both(r):
    return r + turned(r)


def halves(wide):
    high = wide.astype(bf16).astype(f32)
    return jnp.concatenate([high, wide - high], 1).astype(bf16)


def dot(a, b):
    return jnp.dot(a, b, preferred_element_type=f32)


def dot_t(a, b):
    return lax.dot_general(a, b, NT, preferred_element_type=f32)


def kernel(
    near_in, far_in, coarse_in, vec_in, pts_in, bas_in, tra_in, cou_in,
    out_ref,
    near_ref, far_ref, coarse_ref,
    vec, pts, bas, tra, cou, hv, hp, vh, rows, cols, buf_a, buf_b,
    ups, gath, tt, cc, bb, near_out,
    loc, hs, hr, us, ur, zs, zr, ys, yr, cs, cr, chain, here, late,
):
    me = lax.axis_index("leaf")
    zi, yi, ci = me // 16, lax.rem(me // 2, 8), lax.rem(me, 2)
    left, right = me - 1, me + 1
    sibling = me + 1 - 2 * ci

    def y_peer(k):
        return zi * 16 + lax.rem(yi + k, 8) * 2 + ci

    def signal(sem, peer):
        pl.semaphore_signal(sem, inc=1, device_id={"leaf": peer}, device_id_type=MESH)

    beside = [
        (me > 0, me - 1),
        (me < N_LEAF - 1, me + 1),
        (zi > 0, me - 16),
        (zi < 7, me + 16),
    ]
    vi = lax.axis_index("vec")
    first = (me == 0) & (vi == 0)
    after_first = (zi == 0) & (ci == 0) & (yi > 0) & (vi == 0)

    barrier = pltpu.get_barrier_semaphore()

    def greet_y(sem):
        for k in range(1, 8):
            signal(sem, y_peer(k))

    pl.when(jnp.logical_not(first))(functools.partial(greet_y, barrier))
    greeted = 7 - after_first.astype(jnp.int32)
    for there, peer in beside:
        greeted += there.astype(jnp.int32)
        pl.when(there)(functools.partial(signal, barrier, peer))

    locals_ = [
        pltpu.make_async_copy(src, dst, loc.at[i])
        for i, (src, dst) in enumerate(
            [
                (tra_in, tra), (cou_in, cou), (vec_in, vec), (bas_in, bas), (pts_in, pts),
                (near_in, near_ref), (far_in, far_ref), (coarse_in, coarse_ref),
            ]
        )
    ]
    for copy in locals_:
        copy.start()

    def remote(src, dst, send, recv, peer):
        return pltpu.make_async_remote_copy(
            src_ref=src, dst_ref=dst, send_sem=send, recv_sem=recv,
            device_id={"leaf": peer}, device_id_type=MESH,
        )

    to_right = [
        remote(pts_in, hp.at[0], hs.at[1], hr.at[1], right),
        remote(vec_in, hv.at[0], hs.at[0], hr.at[0], right),
    ]
    to_left = [
        remote(pts_in, hp.at[1], hs.at[3], hr.at[3], left),
        remote(vec_in, hv.at[1], hs.at[2], hr.at[2], left),
    ]
    mine = ups.at[NODES:2 * NODES]
    up_right = [remote(mine, ups.at[0:NODES], us.at[0], ur.at[0], right)]
    up_left = [remote(mine, ups.at[2 * NODES:3 * NODES], us.at[1], ur.at[1], left)]

    def run(step, copies):
        for copy in copies:
            getattr(copy, step)()

    def on_core(core, *steps):
        def go():
            for f, *args in steps:
                f(*args)

        pl.when(ci == core)(go)

    def send(rightward, leftward, step):
        def go_right():
            pl.when(me < N_LEAF - 1)(functools.partial(run, step, rightward))

        def go_left():
            pl.when(me > 0)(functools.partial(run, step, leftward))

        on_core(0, (go_left,), (go_right,))
        on_core(1, (go_right,), (go_left,))

    def receive(rightward, leftward):
        pl.when(me > 0)(functools.partial(run, "wait_recv", rightward))
        pl.when(me < N_LEAF - 1)(functools.partial(run, "wait_recv", leftward))

    def lower(f, *args):
        for z in range(7):
            pl.when(z < zi)(functools.partial(f, z, *args))

    def higher(f, *args):
        for z in range(1, 8):
            pl.when(z > zi)(functools.partial(f, z, *args))

    def z_block(core, z):
        return gath.at[z, 0] if core == 0 else gath.at[z, 1, yi]

    def y_block(core, y):
        return gath.at[zi, 0, y] if core == 0 else gath.at[:, 1, y]

    def z_send(to, core, step):
        block = z_block(core, zi)
        run(step, [remote(block, block, zs.at[to], zr.at[zi], to * 16 + yi * 2 + core)])

    def z_receive(source, core):
        block = z_block(core, source)
        peer = source * 16 + yi * 2 + core
        run("wait_recv", [remote(block, block, zs.at[source], zr.at[source], peer)])

    def y_send(core, step):
        block = y_block(core, yi)
        for k in range(1, 8):
            run(step, [remote(block, block, ys.at[k], yr.at[k], y_peer(k))])

    def y_to(k):
        block = y_block(0, yi)
        remote(block, block, ys.at[k], yr.at[k], y_peer(k)).start()

    def y_early():
        for k in range(1, 8):
            put_off = after_first & (lax.rem(yi + k, 8) == 0)
            pl.when(jnp.logical_not(put_off))(functools.partial(y_to, k))

    def y_late():
        @pl.when(after_first)
        def _():
            pl.semaphore_wait(late, 1)
            y_to(8 - yi)

    def y_receive(core):
        for k in range(1, 8):
            block = y_block(core, lax.rem(yi + 8 - k, 8))
            run("wait_recv", [remote(block, block, ys.at[k], yr.at[k], y_peer(8 - k))])

    half, other = gath.at[:, ci], gath.at[:, 1 - ci]
    c_send = remote(half, half, cs, cr, sibling)
    c_receive = remote(other, other, cs, cr, sibling)

    def enter():
        pl.semaphore_wait(barrier, greeted)
        send(to_right, to_left, "start")
        pl.when(first)(functools.partial(greet_y, late))

    pl.when(first)(enter)

    locals_[0].wait()
    for k in range(6):
        for c in range(2):
            tt[k, c * RANK:(c + 1) * RANK, :] = halves(tra[k, c])

    locals_[2].wait()
    locals_[3].wait()
    level = []
    for leaf in range(LEAVES):
        s = stacked(vec[:, leaf * LEAF:(leaf + 1) * LEAF])
        vh[LEAVES + leaf] = jnp.concatenate([s, s], 1)
        b = stacked(bas[leaf])
        bb[leaf] = b
        level.append(both(fold(dot_t(s, b))))
    for k in range(CUT + 1):
        for n, u in enumerate(level):
            packed = pick(u[:8], u[8:])
            if k < CUT:
                ups[NODES + BASE[k] + n] = packed
            else:
                gath[zi, ci, yi] = packed
        if k < CUT:
            lhs = jnp.concatenate(
                [pick(level[2 * n], level[2 * n + 1]) for n in range(len(level) // 2)], 0
            )
            u = both(fold(dot(stacked(lhs), tt[k])))
            level = [u[n * COLS:(n + 1) * COLS] for n in range(len(level) // 2)]
    patient = (yi < 2) & jnp.logical_not(first)

    def greet():
        pl.when(jnp.logical_not(first))(enter)
        on_core(0, (y_early,))
        send(up_right, up_left, "start")

        @pl.when(zi > 0)
        def _():
            pl.semaphore_wait(chain, 1)

        pl.when(zi < 7)(functools.partial(signal, chain, me + 16))
        for z in range(7):
            pl.when(z < zi)(functools.partial(signal, here, z * 16 + yi * 2 + ci))
        on_core(1, (lower, z_send, 1, "start"))

    pl.when(jnp.logical_not(patient))(greet)

    locals_[1].wait()
    for k in range(7):
        for s in range(FAR):
            cc[k, s * RANK:(s + 1) * RANK, :] = halves(cou[k, s])

    def place(m, p):
        x = jnp.broadcast_to(p[0:1, :] * SCALE, (8, LEAF))
        y = jnp.broadcast_to(p[1:2, :] * SCALE, (8, LEAF))
        first = lax.broadcasted_iota(jnp.int32, (8, LEAF), 0) == 0
        cols[m, :, 0:8] = jnp.where(first, x, y).T
        return x, y

    def weights(x, y, m, put):
        x = jnp.concatenate([x] * (STRIP // 8), 0)
        y = jnp.concatenate([y] * (STRIP // 8), 0)
        for r in range(0, LEAF, STRIP):
            sx = jnp.broadcast_to(cols[m, r:r + STRIP, 0:1], (STRIP, LEAF))
            sy = jnp.broadcast_to(cols[m, r:r + STRIP, 1:2], (STRIP, LEAF))
            dx, dy = sx - x, sy - y
            d2 = dx * dx + dy * dy
            if (r // STRIP) % 4 < 3:
                dist = pl.reciprocal(lax.rsqrt(d2), approx=True)
            else:
                d2 = jnp.maximum(d2, TINY)
                dist = d2 * lax.rsqrt(d2)
            put(r, *split(jnp.exp2(-dist)))

    locals_[4].wait()

    def own(i, _):
        for n in range(8):
            t = i * 8 + n
            x, y = place(LEAVES + t, pts[:, pl.ds(pl.multiple_of(t * LEAF, LEAF), LEAF)])
            rows[t, 0] = x
            rows[t, 1] = y
            highs, lows = [], []

            def put(r, high, low):
                highs.append(high)
                lows.append(low)

            weights(x, y, LEAVES + t, put)
            near_out[t] = fold(dot(vh[LEAVES + t], jnp.concatenate(highs + lows, 0)))
        return 0

    def own_part(i, _):
        pl.when((i == 1) & patient)(greet)
        return own(i, _)

    lax.fori_loop(0, LEAVES // 8, own_part, 0)
    for copy in locals_[5:]:
        copy.wait()
    receive(to_right[:1], to_left[:1])

    def others(i, _):
        for n in range(4):
            t = i * 4 + n
            at = pl.ds(pl.multiple_of(t * LEAF, LEAF), LEAF)
            for side in range(2):
                m = 2 * LEAVES * side + t
                place(m, hp[side, :, at])
        return 0

    lax.fori_loop(0, LEAVES // 4, others, 0)

    first_leaf = (me - 1) * LEAVES

    def sources(t):
        return [
            jnp.clip(near_ref[j, t] - first_leaf, 0, 3 * LEAVES - 1) for j in range(NEAR)
        ]

    def weigh(t, buf):
        for j, m in enumerate(sources(t)):
            def put(r, high, low, at=j * 2 * LEAF):
                buf[at + r:at + r + STRIP, :] = high
                buf[at + LEAF + r:at + LEAF + r + STRIP, :] = low

            weights(rows[t, 0], rows[t, 1], m, put)

    def apply(t, buf):
        lhs = jnp.concatenate([vh[m] for m in sources(t)], 1)
        near_out[t] = (near_out[t] + fold(dot(lhs, buf[...]))) * WEIGHT

    weigh(0, buf_a)
    receive(to_right[1:], to_left[1:])

    def parts(i, _):
        for n in range(8):
            t = i * 8 + n
            at = pl.ds(pl.multiple_of(t * LEAF, LEAF), LEAF)
            for side in range(2):
                s = stacked(hv[side, :, at])
                vh[2 * LEAVES * side + t] = jnp.concatenate([s, s], 1)
        return 0

    lax.fori_loop(0, LEAVES // 8, parts, 0)

    def pair(i, _):
        @pl.when(i == 0)
        def _():
            on_core(0, (y_late,), (y_receive, 0), (lower, z_send, 0, "start"))

        @pl.when((i == 2) & (zi < 7))
        def _():
            pl.semaphore_wait(here, 7 - zi)
            on_core(0, (higher, z_send, 0, "start"))
            on_core(1, (higher, z_send, 1, "start"))

        @pl.when(i == 3)
        def _():
            on_core(1, (higher, z_receive, 1), (lower, z_receive, 1), (y_send, 1, "start"))

        @pl.when(i == 6 - 2 * first.astype(jnp.int32))
        def _():
            on_core(0, (higher, z_receive, 0), (lower, z_receive, 0))
            on_core(1, (y_receive, 1))
            c_send.start()

        apply(2 * i, buf_a)
        weigh(2 * i + 1, buf_b)
        apply(2 * i + 1, buf_b)
        weigh(2 * i + 2, buf_a)
        return 0

    lax.fori_loop(0, LEAVES // 2 - 1, pair, 0)

    receive(up_right, up_left)
    c_receive.wait_recv()
    apply(LEAVES - 2, buf_a)
    weigh(LEAVES - 1, buf_b)

    def four(xs):
        rs = [turned(x) for x in xs]
        return jnp.concatenate(
            [
                jnp.concatenate([pick(xs[s], rs[s + 1]), pick(rs[s], xs[s + 1])], 0)
                for s in (0, 2)
            ],
            1,
        )

    def cut_node(n):
        return gath[n >> 4, n & 1, (n >> 1) & 7]

    def couple(lhs, k):
        return both(fold(dot(stacked(lhs), cc[k])))

    far = []
    for k in range(CUT):
        span = LEAVES >> k
        base = (me - 1) * span
        blocks = []
        for n in range(span):
            xs = []
            for s in range(FAR):
                at = jnp.clip(far_ref[k, s, n] - base, 0, 3 * span - 1)
                side = at >> (CUT - k)
                xs.append(ups[at + side * (NODES - span) + BASE[k]])
            blocks.append(four(xs))
        far.append(couple(jnp.concatenate(blocks, 0), k))

    far_4 = couple(four([cut_node(coarse_ref[0, s, me]) for s in range(FAR)]), 4)

    def joined(n):
        a, b = cut_node(2 * n), cut_node(2 * n + 1)
        return jnp.concatenate([pick(a, turned(b)), pick(turned(a), b)], 0)

    mid, top = me // 2, me // 4
    blocks = [joined(coarse_ref[1, s, mid]) for s in range(FAR)]
    for s in range(FAR):
        n = coarse_ref[2, s, top]
        blocks += [joined(2 * n), joined(2 * n + 1)]
    u = both(fold(dot(stacked(jnp.concatenate(blocks, 0)), tt[4])))
    u = [u[n * COLS:(n + 1) * COLS] for n in range(12)]
    far_5 = couple(jnp.concatenate([pick(u[0], u[1]), pick(u[2], u[3])], 1), 5)
    lhs = jnp.concatenate([pick(u[4 + 2 * s], u[5 + 2 * s]) for s in range(FAR)], 0)
    u = both(fold(dot(stacked(lhs), tt[5])))
    u = [u[n * COLS:(n + 1) * COLS] for n in range(4)]
    down = couple(jnp.concatenate([pick(u[0], u[1]), pick(u[2], u[3])], 1), 6)

    def children(d, k):
        r = fold(dot_t(stacked(d), tt[k]))
        t = turned(r)
        return pick(r, t), pick(t, r)

    for k, node, here in ((5, mid, far_5), (4, me, far_4)):
        a, b = children(down, k)
        down = here + jnp.where(lax.rem(node, 2) == 0, a, b)
    for k in range(CUT - 1, -1, -1):
        a, b = children(down, k)
        parts = []
        for n in range(a.shape[0] // COLS):
            at = slice(n * COLS, (n + 1) * COLS)
            parts += [a[at], b[at]]
        down = far[k] + jnp.concatenate(parts, 0)

    apply(LEAVES - 1, buf_b)
    for leaf in range(LEAVES):
        d = stacked(down[leaf * COLS:(leaf + 1) * COLS])
        out_ref[leaf] = near_out[leaf] + fold(dot(d, bb[leaf]))

    send(to_right, to_left, "wait_send")
    send(up_right, up_left, "wait_send")
    for core in range(2):
        on_core(
            core,
            (lower, z_send, core, "wait_send"),
            (higher, z_send, core, "wait_send"),
            (y_send, core, "wait_send"),
        )
    c_send.wait_send()


def local(vectors, points, bases, transfer, coupling, near_lists, far_lists, coarse_lists):
    outside = pl.BlockSpec(memory_space=pltpu.HBM)
    smem = pltpu.SMEM
    vmem = pltpu.VMEM
    dma = pltpu.SemaphoreType.DMA
    by_leaf = pl.pallas_call(
        kernel,
        out_shape=jax.ShapeDtypeStruct((LEAVES, COLS, LEAF), f32),
        in_specs=[outside] * 8,
        out_specs=pl.BlockSpec(memory_space=vmem),
        scratch_shapes=[
            smem((NEAR, LEAVES), jnp.int32),
            smem((CUT, FAR, LEAVES), jnp.int32),
            smem((3, FAR, N_LEAF), jnp.int32),
            vmem((COLS, LEAVES * LEAF), f32),
            vmem((2, LEAVES * LEAF), f32),
            vmem((LEAVES, RANK, LEAF), f32),
            vmem((6, 2, RANK, RANK), f32),
            vmem((7, FAR, RANK, RANK), f32),
            vmem((2, COLS, LEAVES * LEAF), f32),
            vmem((2, 2, LEAVES * LEAF), f32),
            vmem((3 * LEAVES, 2 * COLS, 2 * LEAF), bf16),
            vmem((LEAVES, 2, 8, LEAF), f32),
            vmem((3 * LEAVES, LEAF, 128), f32),
            vmem((NEAR * 2 * LEAF, LEAF), bf16),
            vmem((NEAR * 2 * LEAF, LEAF), bf16),
            vmem((3 * NODES, 8, 128), f32),
            vmem((8, 2, 8, 8, 128), f32),
            vmem((6, 2 * RANK, 2 * RANK), bf16),
            vmem((7, FAR * RANK, 2 * RANK), bf16),
            vmem((LEAVES, 2 * RANK, LEAF), bf16),
            vmem((LEAVES, COLS, LEAF), f32),
            dma((8,)), dma((4,)), dma((4,)), dma((2,)), dma((2,)),
            dma((8,)), dma((8,)), dma((8,)), dma((8,)), dma, dma,
            pltpu.SemaphoreType.REGULAR, pltpu.SemaphoreType.REGULAR,
            pltpu.SemaphoreType.REGULAR,
        ],
        compiler_params=pltpu.CompilerParams(
            collective_id=0, has_side_effects=True, vmem_limit_bytes=62 * 2**20
        ),
    )(
        near_lists.T,
        far_lists.transpose(0, 2, 1),
        coarse_lists.transpose(0, 2, 1),
        vectors,
        points,
        bases.transpose(0, 2, 1),
        transfer,
        coupling,
    )
    return by_leaf.transpose(1, 0, 2).reshape(vectors.shape)


def solution(mesh):
    in_specs = (
        P("vec", "leaf"),
        P(None, "leaf"),
        P("leaf", None, None),
        P(),
        P(),
        P("leaf", None),
        P(None, "leaf", None),
        P(),
    )
    return jax.shard_map(
        local, mesh=mesh, in_specs=in_specs, out_specs=P("vec", "leaf"), check_vma=False
    )
```
